32 devices in a mesh: seq: 4 (over y, x), dp: 8 (over z, core).
Axes of the slice: x: 2, y: 2, z: 4, core: 2. Of those that a mesh axis runs over, the one named last changes fastest.
Arguments:
- tokens: bfloat16 [8, 2048, 1024], P('dp', 'seq'), may hold values from -6 to 6
- cotangent: bfloat16 [8, 2048, 1024], P('dp', 'seq'), may hold values from -6 to 6
- block_order: int32 [8, 4], P('dp'), may hold values from 0 to 3, each once within a row
- joint_weight: bfloat16 [1024, 3072], P(('seq', 'dp')), may hold values from -0.1875 to 0.1875
- query_bias: bfloat16 [1024], P(('seq', 'dp')), may hold values from -3 to 3
- value_bias: bfloat16 [1024], P(('seq', 'dp')), may hold values from -3 to 3
- projection: bfloat16 [1024, 1024], P(('seq', 'dp')), may hold values from -0.75 to 0.75
- offset: bfloat16 [1024], P(('seq', 'dp')), may hold values from -3 to 3
- first_gain: bfloat16 [1024], P(('seq', 'dp')), may hold values from 0.099609375 to 1.8984375
- first_shift: bfloat16 [1024], P(('seq', 'dp')), may hold values from -3 to 3
- upward_weight: bfloat16 [1024, 4096], P(('seq', 'dp')), may hold values from -0.1875 to 0.1875
- upward_bias: bfloat16 [4096], P(('seq', 'dp')), may hold values from -3 to 3
- downward_weight: bfloat16 [4096, 1024], P(('seq', 'dp')), may hold values from -0.09375 to 0.09375
- downward_bias: bfloat16 [1024], P(('seq', 'dp')), may hold values from -3 to 3
- second_gain: bfloat16 [1024], P(('seq', 'dp')), may hold values from 0.099609375 to 1.8984375
- second_shift: bfloat16 [1024], P(('seq', 'dp')), may hold values from -3 to 3
Outputs:
- output: bfloat16 [8, 2048, 1024], P('dp', 'seq')
- input_grad: bfloat16 [8, 2048, 1024], P('dp', 'seq')
- joint_grad: float32 [1024, 3072], P(('seq', 'dp'))
- query_grad: float32 [1024], P(('seq', 'dp'))
- value_grad: float32 [1024], P(('seq', 'dp'))
- projection_grad: float32 [1024, 1024], P(('seq', 'dp'))
- offset_grad: float32 [1024], P(('seq', 'dp'))
- firstgain_grad: float32 [1024], P(('seq', 'dp'))
- firstshift_grad: float32 [1024], P(('seq', 'dp'))
- upward_grad: float32 [1024, 4096], P(('seq', 'dp'))
- upwardbias_grad: float32 [4096], P(('seq', 'dp'))
- downward_grad: float32 [4096, 1024], P(('seq', 'dp'))
- downwardbias_grad: float32 [1024], P(('seq', 'dp'))
- secondgain_grad: float32 [1024], P(('seq', 'dp'))
- secondshift_grad: float32 [1024], P(('seq', 'dp'))
The draws below stay inside these ranges and needn't reach their ends.
Inputs may be any that keep to these rules, and one draw needn't show every extreme that they name: Each row is an ordering of the 4 position blocks of one sequence: index j of seq holds block block_order[s, j].
All inputs are finite; a program needn't handle non-finite values.
Results may differ from the reference program's by a relative error of at most 0.02.
Values may be sent and summed in bfloat16 or wider, within the bound.
No kernel may reach another device: no remote copies, remote signals or barrier semaphores. Data moves between devices by JAX's collectives and lax.ppermute only.
A program may use at most 256 MiB of HBM per device.

```python
import math
import jax
import jax.numpy as jnp
from jax import lax

D = 1024
HEADS = 16
HEAD_DIM = 64
FF = 4096
BLK = 512
SEQS = 8
SEQ_LEN = 2048
N_SEQ = 4


def block_levels(rng, shape, shards, least, top_value):
    def one(position, blocks):
        draws = jax.random.uniform(jax.random.fold_in(jax.random.fold_in(rng, 6), position), (blocks,), jnp.float32, least / len(shards), top_value / len(shards))
        return jnp.repeat(jnp.exp(draws), shape[position] // blocks).reshape((-1,) + (1,) * (len(shape) - position - 1))

    factor_of = one(*shards[0])
    for cut in shards[1:]:
        factor_of = factor_of * one(*cut)
    return factor_of


def normal_values(key, extent, spread, limit, shards=(), kind=jnp.bfloat16):
    level = block_levels(key, extent, shards, -0.22, 0.18) if shards else 1.0
    values = jax.random.normal(key, extent, jnp.float32) * spread * level
    return jnp.minimum(jnp.maximum(values, -limit), limit).astype(kind)


def setup_inputs(seed: int = 0) -> dict:
    key_list = jax.random.split(jax.random.key(seed), 17)
    return {
        "tokens": normal_values(key_list[0], (SEQS, SEQ_LEN, D), 1.0, 6.0, ((0, 8), (1, 4))),
        "cotangent": normal_values(key_list[1], (SEQS, SEQ_LEN, D), 1.0, 6.0, ((0, 8), (1, 4))),
        "block_order": jax.vmap(lambda own: jax.random.permutation(own, N_SEQ))(jax.random.split(key_list[2], SEQS)).reshape((SEQS, N_SEQ)).astype(jnp.int32),
        "joint_weight": normal_values(key_list[3], (D, 3 * D), D ** -0.5, 0.1875, ((0, 32),)),
        "query_bias": normal_values(key_list[4], (D,), 0.5, 3.0, ((0, 32),)),
        "value_bias": normal_values(key_list[5], (D,), 0.5, 3.0, ((0, 32),)),
        "projection": normal_values(key_list[6], (D, D), (D // 16) ** -0.5, 0.75, ((0, 32),)),
        "offset": normal_values(key_list[7], (D,), 0.5, 3.0, ((0, 32),)),
        "first_gain": jnp.clip(1.0 + 0.18 * jax.random.normal(key_list[8], (D,), jnp.float32), 0.099609375, 1.8984375).astype(jnp.bfloat16),
        "first_shift": normal_values(key_list[9], (D,), 0.5, 3.0, ((0, 32),)),
        "upward_weight": normal_values(key_list[10], (D, FF), D ** -0.5, 0.1875, ((0, 32),)),
        "upward_bias": normal_values(key_list[11], (FF,), 0.5, 3.0, ((0, 32),)),
        "downward_weight": normal_values(key_list[12], (FF, D), FF ** -0.5, 0.09375, ((0, 32),)),
        "downward_bias": normal_values(key_list[13], (D,), 0.5, 3.0, ((0, 32),)),
        "second_gain": jnp.clip(1.0 + 0.18 * jax.random.normal(key_list[14], (D,), jnp.float32), 0.099609375, 1.8984375).astype(jnp.bfloat16),
        "second_shift": normal_values(key_list[15], (D,), 0.5, 3.0, ((0, 32),)),
    }


@jax.custom_vjp
def low(v):
    return lax.optimization_barrier(v.astype(jnp.bfloat16)).astype(jnp.float32)

@jax.custom_vjp
def low_back(v):
    return v

def low_keep(v):
    return (low(v), None)

def low_pass(kept, grad):
    return (grad,)

def back_keep(v):
    return (v, None)

def back_low(kept, grad):
    return (low(grad),)
low.defvjp(low_keep, low_pass)
low_back.defvjp(back_keep, back_low)
epsilon = 1e-05
masked_score = -1e+30

def both_ways(values):
    return low_back(low(values))

def layer_norm(values, scaling, shifting):
    average = lax.optimization_barrier(jnp.mean(values, -1, keepdims=True))
    centered = values - average
    variance = lax.optimization_barrier(jnp.mean(centered * centered, -1, keepdims=True))
    return centered * lax.rsqrt(variance + epsilon) * scaling + shifting

def product(left, right):
    return jnp.dot(left, right, precision=lax.Precision.HIGHEST)

def layer(values, params, places):
    joint, query_add, value_add, projection, offset, gain_one, shift_one, upward, upward_add, downward, downward_add, gain_two, shift_two = params
    total = values.shape[0]
    normed = low(layer_norm(values, gain_one, shift_one))
    mixture = product(normed, joint)
    queries = both_ways(mixture[:, :D] + query_add).reshape(total, HEADS, HEAD_DIM)
    keyset = both_ways(mixture[:, D:2 * D]).reshape(total, HEADS, HEAD_DIM)
    valueset = both_ways(mixture[:, 2 * D:] + value_add).reshape(total, HEADS, HEAD_DIM)
    slopes = 2.0 ** (-8.0 * (jnp.arange(HEADS, dtype=jnp.float32) + 1.0) / HEADS) * (4.0 / SEQ_LEN)
    factor = 1.0 / math.sqrt(HEAD_DIM)

    def attend(inputs):
        block_queries, block_places = inputs
        products = jnp.einsum('qhe,khe->hqk', block_queries, keyset, precision=lax.Precision.HIGHEST) * factor
        distance = (places[None, :] - block_places[:, None]).astype(jnp.float32)
        allowed = places[None, :] <= block_places[:, None]
        scores = jnp.where(allowed[None], products + slopes[:, None, None] * distance[None], masked_score)
        scores = low_back(scores)
        weights = jax.nn.softmax(scores, axis=-1)
        return jnp.einsum('hqk,khe->qhe', low(weights), valueset, precision=lax.Precision.HIGHEST)
    attended = lax.map(jax.checkpoint(attend), (queries.reshape(total // BLK, BLK, HEADS, HEAD_DIM), places.reshape(total // BLK, BLK)))
    attended = both_ways(attended.reshape(total, D))
    branch = low_back(product(attended, projection) + offset)
    middle = values + branch
    second = low(layer_norm(middle, gain_two, shift_two))
    hidden = low_back(product(second, upward) + upward_add)
    active = low(jax.nn.gelu(hidden, approximate=True))
    result = low_back(product(active, downward) + downward_add)
    return middle + result

def reference(tokens, cotangent, block_order, joint_weight, query_bias, value_bias, projection, offset, first_gain, first_shift, upward_weight, upward_bias, downward_weight, downward_bias, second_gain, second_shift):
    params = tuple((weight.astype(jnp.float32) for weight in (joint_weight, query_bias, value_bias, projection, offset, first_gain, first_shift, upward_weight, upward_bias, downward_weight, downward_bias, second_gain, second_shift)))

    def one_sequence(carried, inputs):
        sequence, sequence_grad, ordering = inputs
        places = (ordering[:, None] * BLK + jnp.arange(BLK, dtype=jnp.int32)[None, :]).reshape(-1).astype(jnp.int32)

        def forward(values, weights):
            return layer(values, weights, places)
        result, pullback = jax.vjp(forward, sequence.astype(jnp.float32), params)
        grad_values, grad_params = pullback(sequence_grad.astype(jnp.float32))
        carried = jax.tree.map(jnp.add, carried, grad_params)
        return (carried, (result.astype(jnp.bfloat16), grad_values.astype(jnp.bfloat16)))
    zeros = tuple((jnp.zeros_like(weight) for weight in params))
    grads, (outputs, input_grads) = lax.scan(one_sequence, zeros, (tokens, cotangent, block_order))
    return (outputs, input_grads, grads[0], grads[1], grads[2], grads[3], grads[4], grads[5], grads[6], grads[7], grads[8], grads[9], grads[10], grads[11], grads[12])
```

```python
import math
from functools import partial

import jax
import jax.numpy as jnp
from jax import lax
from jax.experimental import pallas as pl
from jax.experimental.pallas import tpu as pltpu
from jax.sharding import PartitionSpec as P

HEADS = 16
EVERY = ("seq", "dp")
LOG2E = math.log2(math.e)
epsilon = 1e-05
lowest = -1e30
bf16 = jnp.bfloat16
f32 = jnp.float32


def layer_norm(values, scaling, shifting):
    average = jnp.mean(values, -1, keepdims=True)
    centered = values - average
    variance = jnp.mean(centered * centered, -1, keepdims=True)
    return centered * lax.rsqrt(variance + epsilon) * scaling + shifting


def gelu_tanh(values):
    return jax.nn.gelu(values, approximate=True)


def matmul(left, right):
    return jnp.dot(left, right, preferred_element_type=f32)


def left_transposed(left, right):
    return lax.dot_general(left, right, (((0,), (0,)), ((), ())), preferred_element_type=f32)


def right_transposed(left, right):
    return lax.dot_general(left, right, (((1,), (1,)), ((), ())), preferred_element_type=f32)


def sizes():
    return lax.axis_size("seq"), lax.axis_size("dp") // 2


def places():
    dp = lax.axis_index("dp")
    return lax.axis_index("seq"), dp // 2, dp % 2


def to_core(value):
    count = lax.axis_size("dp")
    return lax.ppermute(value, "dp", [(i, i ^ 1) for i in range(count)])


def to_seq(value, by):
    count = lax.axis_size("seq")
    return lax.ppermute(value, "seq", [(i, i ^ by) for i in range(count)])


def to_z(value, by):
    count = lax.axis_size("dp")
    return lax.ppermute(value, "dp", [(i, (i + 2 * by) % count) for i in range(count)])


def put_in_order(pieces):
    count = len(pieces)
    nz, rows, columns = pieces[0].shape
    total = count * nz

    def kernel(place, *refs):
        ins, out, held, in_sem, out_sem = refs[:count], *refs[count:]
        copies = []
        for p in range(count):
            for t in range(nz):
                slot = p * nz + t
                copy = pltpu.make_async_copy(ins[p].at[t], held.at[slot], in_sem.at[slot])
                copy.start()
                copies.append(copy)
        outs = []
        for p in range(count):
            for t in range(nz):
                slot = p * nz + t
                z = lax.rem(place[1] - t + nz, nz)
                owner = ((place[0] ^ (p // 2)) * nz + z) * 2 + (place[2] ^ (p % 2))
                copies[slot].wait()
                copy = pltpu.make_async_copy(held.at[slot], out.at[owner], out_sem.at[slot])
                copy.start()
                outs.append(copy)
        for copy in outs:
            copy.wait()

    size = total * rows * columns * 2
    return pl.pallas_call(
        kernel,
        name="put_in_order",
        out_shape=jax.ShapeDtypeStruct((total, rows, columns), pieces[0].dtype),
        in_specs=[pl.BlockSpec(memory_space=pltpu.SMEM)]
        + [pl.BlockSpec(memory_space=pl.ANY)] * count,
        out_specs=pl.BlockSpec(memory_space=pl.ANY),
        scratch_shapes=[
            pltpu.VMEM((total, rows, columns), pieces[0].dtype),
            pltpu.SemaphoreType.DMA((total,)),
            pltpu.SemaphoreType.DMA((total,)),
        ],
        compiler_params=pltpu.CompilerParams(vmem_limit_bytes=size + (4 << 20)),
        cost_estimate=pl.CostEstimate(flops=0, bytes_accessed=2 * size, transcendentals=0),
    )(jnp.stack(places()).astype(jnp.int32), *pieces).reshape(total * rows, columns)


def gathered(shard):
    ns, nz = sizes()
    column = jnp.stack([shard] + [to_z(shard, by) for by in range(1, nz)])
    planes = [column] + [to_seq(column, by) for by in range(1, ns)]
    pieces = []
    for plane in planes:
        pieces += [plane, to_core(plane)]
    return put_in_order(pieces)


def scattered(grad):
    ns, nz = sizes()
    seq, z, core = places()
    columns = grad.shape[1]
    blocks = grad.reshape(ns, nz, 2, -1, columns)
    mine = lax.dynamic_index_in_dim(blocks, core, 2, keepdims=False)
    other = lax.dynamic_index_in_dim(blocks, 1 - core, 2, keepdims=False)
    chip = (mine.astype(f32) + to_core(other.astype(bf16)).astype(f32)).astype(bf16)
    total = lax.dynamic_index_in_dim(chip, seq, 0, keepdims=False).astype(f32)
    for by in range(1, ns):
        piece = lax.dynamic_index_in_dim(chip, seq ^ by, 0, keepdims=False)
        total = total + to_seq(piece, by).astype(f32)
    plane = total.astype(bf16)
    total = lax.dynamic_index_in_dim(plane, z, 0, keepdims=False).astype(f32)
    for by in range(1, nz):
        piece = lax.dynamic_index_in_dim(plane, (z + by) % nz, 0, keepdims=False)
        total = total + to_z(piece, by).astype(f32)
    return total


def half_lanes(shape, which):
    lane = lax.broadcasted_iota(jnp.int32, shape, len(shape) - 1)
    return (lane < 64) if which == 0 else (lane >= 64)


def with_bias(keys, slope, first_place, which):
    lane = lax.broadcasted_iota(jnp.int32, keys.shape, 1) - (64 if which == 0 else 0)
    row = lax.broadcasted_iota(jnp.int32, keys.shape, 0) + first_place
    bias = row.astype(f32) * (slope * 8.0)
    high = bias.astype(bf16)
    rest = bias - high.astype(f32)
    middle = rest.astype(bf16)
    low = (rest - middle.astype(f32)).astype(bf16)
    zero = jnp.zeros_like(high)
    terms = jnp.where(
        lane == 0, high, jnp.where(lane == 1, middle, jnp.where(lane == 2, low, zero))
    )
    return jnp.where(half_lanes(keys.shape, which), keys, terms)


def attention_forward(qkv, order, slopes):
    ns, _, length, width = qkv.shape
    pairs = width // 128
    scale = LOG2E / 8.0

    def kernel(order_ref, slope_ref, q_ref, kv_ref, low_ref, full_ref, log_ref):
        pair, place = pl.program_id(0), pl.program_id(1)
        shape = (length, 128)
        queries = [
            jnp.where(half_lanes(shape, w), q_ref[0, 0], jnp.ones(shape, bf16)) for w in (0, 1)
        ]

        def step(block, state, diagonal):
            at = order_ref[block]
            result = []
            for w in (0, 1):
                top, acc = state[w]
                keys = with_bias(kv_ref[at, 1], slope_ref[pair * 2 + w], block * length, w)
                scores = right_transposed(keys, queries[w])
                if diagonal:
                    k = lax.broadcasted_iota(jnp.int32, scores.shape, 0)
                    q = lax.broadcasted_iota(jnp.int32, scores.shape, 1)
                    scores = jnp.where(k <= q, scores, lowest)
                new_top = jnp.maximum(top, jnp.max(scores, 0, keepdims=True))
                weights = jnp.exp2(scores * scale - new_top * scale).astype(bf16)
                values = jnp.where(half_lanes(shape, w), kv_ref[at, 2], jnp.ones(shape, bf16))
                acc = acc * jnp.exp2((top - new_top) * scale) + left_transposed(values, weights)
                result.append((new_top, acc))
            return tuple(result)

        start = (jnp.full((1, length), lowest, f32), jnp.zeros((128, length), f32))
        state = lax.fori_loop(
            0, place, lambda block, state: step(block, state, False), (start, start)
        )
        (top0, acc0), (top1, acc1) = step(place, state, True)
        sum0, sum1 = acc0[64:65], acc1[0:1]
        row = lax.broadcasted_iota(jnp.int32, (128, length), 0)
        attended = jnp.where(row < 64, acc0 / sum0, acc1 / sum1).T
        full_ref[0] = attended
        low_ref[0] = attended.astype(bf16)
        row = lax.broadcasted_iota(jnp.int32, (8, length), 0)
        log_ref[0, 0] = jnp.where(
            row == 0, top0 * scale + jnp.log2(sum0), top1 * scale + jnp.log2(sum1)
        )

    per_block = 2 * 2 * length * length * 128 * 2
    grid_spec = pltpu.PrefetchScalarGridSpec(
        num_scalar_prefetch=2,
        grid=(pairs, ns),
        in_specs=[
            pl.BlockSpec((1, 1, length, 128), lambda p, i, order, slope: (order[i], 0, 0, p)),
            pl.BlockSpec((ns, 3, length, 128), lambda p, i, order, slope: (0, 0, 0, p)),
        ],
        out_specs=[
            pl.BlockSpec((1, length, 128), lambda p, i, order, slope: (order[i], 0, p)),
            pl.BlockSpec((1, length, 128), lambda p, i, order, slope: (order[i], 0, p)),
            pl.BlockSpec((1, 1, 8, length), lambda p, i, order, slope: (p, i, 0, 0)),
        ],
    )
    return pl.pallas_call(
        kernel,
        name="attention_forward",
        grid_spec=grid_spec,
        out_shape=[
            jax.ShapeDtypeStruct((ns, length, width), bf16),
            jax.ShapeDtypeStruct((ns, length, width), f32),
            jax.ShapeDtypeStruct((pairs, ns, 8, length), f32),
        ],
        compiler_params=pltpu.CompilerParams(vmem_limit_bytes=40 << 20),
        cost_estimate=pl.CostEstimate(
            flops=pairs * per_block * ns * (ns + 1) // 2 * 4,
            bytes_accessed=qkv.size * 2 + ns * length * width * 6,
            transcendentals=pairs * ns * (ns + 1) * length * length,
        ),
    )(order, slopes, qkv, qkv)


def attention_backward(qkv, grad, full, logs, order, slopes):
    ns, _, length, width = qkv.shape
    pairs = width // 128
    scale = LOG2E / 8.0

    def kernel(
        order_ref, slope_ref, qkv_ref, grad_ref, full_ref, log_ref, out_ref, dq_ref, delta_ref
    ):
        pair, block = pl.program_id(0), pl.program_id(1)
        shape = (length, 128)

        @pl.when(block == 0)
        def _():
            def one(i, _):
                at = order_ref[i]
                product = (grad_ref[at].astype(f32) * full_ref[at]).T
                delta_ref[i] = jnp.concatenate(
                    [
                        jnp.sum(product[:64], 0, keepdims=True),
                        jnp.sum(product[64:], 0, keepdims=True),
                    ],
                    0,
                )
                dq_ref[i] = jnp.zeros((128, length), f32)
                return 0

            lax.fori_loop(0, ns, one, 0)

        here = order_ref[block]
        keys, values = qkv_ref[here, 1], qkv_ref[here, 2]
        zero = jnp.zeros(shape, bf16)
        one = jnp.ones(shape, bf16)
        masks = [half_lanes(shape, w) for w in (0, 1)]
        biased = [
            with_bias(keys, slope_ref[pair * 2 + w], block * length, w) for w in (0, 1)
        ]
        own_keys = [jnp.where(masks[w], keys, zero) for w in (0, 1)]
        own_values = [jnp.where(masks[w], values, zero) for w in (0, 1)]

        def step(i, state, diagonal):
            at = order_ref[i]
            grad_keys, grad_values = state
            queries, grads = qkv_ref[at, 0], grad_ref[at]
            grad_queries = dq_ref[i]
            for w in (0, 1):
                scores = right_transposed(biased[w], jnp.where(masks[w], queries, one))
                weights = jnp.exp2(scores * scale - log_ref[0, i, w : w + 1])
                if diagonal:
                    k = lax.broadcasted_iota(jnp.int32, scores.shape, 0)
                    q = lax.broadcasted_iota(jnp.int32, scores.shape, 1)
                    weights = jnp.where(k <= q, weights, 0.0)
                grad_weights = right_transposed(own_values[w], grads)
                grad_scores = (weights * (grad_weights - delta_ref[i, w : w + 1])).astype(bf16)
                own_grads = jnp.where(masks[w], grads, zero)
                own_queries = jnp.where(masks[w], queries, zero)
                grad_values = grad_values + matmul(weights.astype(bf16), own_grads)
                grad_keys = grad_keys + matmul(grad_scores, own_queries)
                grad_queries = grad_queries + left_transposed(own_keys[w], grad_scores)
            dq_ref[i] = grad_queries
            return grad_keys, grad_values

        start = (jnp.zeros(shape, f32), jnp.zeros(shape, f32))
        state = step(block, start, True)
        grad_keys, grad_values = lax.fori_loop(
            block + 1, ns, lambda i, state: step(i, state, False), state
        )
        out_ref[here, 1] = (grad_keys * 0.125).astype(bf16)
        out_ref[here, 2] = grad_values.astype(bf16)
        out_ref[here, 0] = (dq_ref[block].T * 0.125).astype(bf16)

    per_block = 2 * 5 * length * length * 128 * 2
    grid_spec = pltpu.PrefetchScalarGridSpec(
        num_scalar_prefetch=2,
        grid=(pairs, ns),
        in_specs=[
            pl.BlockSpec((ns, 3, length, 128), lambda p, i, order, slope: (0, 0, 0, p)),
            pl.BlockSpec((ns, length, 128), lambda p, i, order, slope: (0, 0, p)),
            pl.BlockSpec((ns, length, 128), lambda p, i, order, slope: (0, 0, p)),
            pl.BlockSpec((1, ns, 8, length), lambda p, i, order, slope: (p, 0, 0, 0)),
        ],
        out_specs=pl.BlockSpec((ns, 3, length, 128), lambda p, i, order, slope: (0, 0, 0, p)),
        scratch_shapes=[
            pltpu.VMEM((ns, 128, length), f32),
            pltpu.VMEM((ns, 2, length), f32),
        ],
    )
    return pl.pallas_call(
        kernel,
        name="attention_backward",
        grid_spec=grid_spec,
        out_shape=jax.ShapeDtypeStruct((ns, 3, length, width), bf16),
        compiler_params=pltpu.CompilerParams(vmem_limit_bytes=48 << 20),
        cost_estimate=pl.CostEstimate(
            flops=pairs * per_block * ns * (ns + 1) // 2 * 4,
            bytes_accessed=qkv.size * 4 + ns * length * width * 6,
            transcendentals=pairs * ns * (ns + 1) * length * length,
        ),
    )(order, slopes, qkv, grad, full, logs)


def body(
    tokens,
    cotangent,
    block_order,
    joint_weight,
    query_bias,
    value_bias,
    projection,
    offset,
    first_gain,
    first_shift,
    upward_weight,
    upward_bias,
    downward_weight,
    downward_bias,
    second_gain,
    second_shift,
):
    members, length, features = tokens.shape
    ns, nz = sizes()
    seq = lax.axis_index("seq")
    width = features // ns
    group = HEADS // ns
    devices = ns * nz * 2

    small = (
        query_bias,
        value_bias,
        offset,
        first_gain,
        first_shift,
        upward_bias,
        downward_bias,
        second_gain,
        second_shift,
    )
    packed = lax.all_gather(jnp.concatenate(small)[None], EVERY, axis=0, tiled=True)
    smalls, first = [], 0
    for one in small:
        smalls.append(packed[:, first : first + one.shape[0]].reshape(-1).astype(f32))
        first += one.shape[0]
    (
        query_add,
        value_add,
        offset_add,
        gain_one,
        shift_one,
        upward_add,
        downward_add,
        gain_two,
        shift_two,
    ) = smalls

    joint_full = gathered(joint_weight)
    projection_full = gathered(projection)
    upward_full = gathered(upward_weight)
    downward_full = gathered(downward_weight)

    slopes = 2.0 ** (-8.0 * (jnp.arange(HEADS, dtype=f32) + 1.0) / HEADS) * (4.0 / (length * ns))
    slopes = lax.dynamic_slice_in_dim(slopes, seq * group, group)
    order = jnp.argsort(block_order[0]).astype(jnp.int32)

    inputs = tokens.reshape(length, features).astype(f32)
    normed, first_pull = jax.vjp(layer_norm, inputs, gain_one, shift_one)
    normed_low = normed.astype(bf16)
    zeros = jnp.zeros_like(query_add)
    mixture = matmul(normed_low, joint_full) + jnp.concatenate([query_add, zeros, value_add])
    mixture = mixture.astype(bf16).reshape(length, 3, ns, width).transpose(2, 1, 0, 3)
    qkv = lax.all_to_all(mixture, "seq", 0, 0, tiled=True)
    attended, attended_full, logs = attention_forward(qkv, order, slopes)
    attended = lax.all_to_all(attended, "seq", 0, 0, tiled=True)
    attended_low = attended.transpose(1, 0, 2).reshape(length, features)

    middle = inputs + matmul(attended_low, projection_full) + offset_add
    second, second_pull = jax.vjp(layer_norm, middle, gain_two, shift_two)
    second_low = second.astype(bf16)
    hidden = matmul(second_low, upward_full) + upward_add
    active, gelu_pull = jax.vjp(gelu_tanh, hidden)
    active_low = active.astype(bf16)
    result = matmul(active_low, downward_full) + downward_add
    output = (middle + result).astype(bf16).reshape(members, length, features)

    grad_result = cotangent.reshape(length, features)
    grad_result_full = grad_result.astype(f32)
    downward_grad = left_transposed(active_low, grad_result)
    downwardbias_grad = jnp.sum(grad_result_full, 0)
    (grad_hidden,) = gelu_pull(right_transposed(grad_result, downward_full))
    grad_hidden_low = grad_hidden.astype(bf16)
    upward_grad = left_transposed(second_low, grad_hidden_low)
    upwardbias_grad = jnp.sum(grad_hidden_low.astype(f32), 0)
    grad_second = right_transposed(grad_hidden_low, upward_full)
    middle_part, secondgain_grad, secondshift_grad = second_pull(grad_second)
    downward_sum = scattered(downward_grad)
    upward_sum = scattered(upward_grad)

    grad_middle = grad_result_full + middle_part
    grad_branch = grad_middle.astype(bf16)
    projection_sum = scattered(left_transposed(attended_low, grad_branch))
    offset_grad = jnp.sum(grad_branch.astype(f32), 0)
    grad_attended = right_transposed(grad_branch, projection_full).astype(bf16)
    grad_attended = grad_attended.reshape(length, ns, width).transpose(1, 0, 2)
    grad_attended = lax.all_to_all(grad_attended, "seq", 0, 0, tiled=True)
    grad_qkv = attention_backward(qkv, grad_attended, attended_full, logs, order, slopes)
    grad_qkv = lax.all_to_all(grad_qkv, "seq", 0, 0, tiled=True)
    grad_mixture = grad_qkv.transpose(2, 1, 0, 3).reshape(length, 3 * features)
    joint_sum = scattered(left_transposed(normed_low, grad_mixture))
    mixture_sums = jnp.sum(grad_mixture.astype(f32), 0)
    grad_normed = right_transposed(grad_mixture, joint_full)
    input_part, firstgain_grad, firstshift_grad = first_pull(grad_normed)
    input_grad = (grad_middle + input_part).astype(bf16).reshape(members, length, features)

    grads = (
        mixture_sums[:features],
        mixture_sums[2 * features :],
        offset_grad,
        firstgain_grad,
        firstshift_grad,
        upwardbias_grad,
        downwardbias_grad,
        secondgain_grad,
        secondshift_grad,
    )
    packed = jnp.concatenate([g.reshape(devices, -1) for g in grads], 1)
    packed = lax.psum_scatter(packed, EVERY, scatter_dimension=0, tiled=True)[0]
    sums, first = [], 0
    for one in small:
        sums.append(packed[first : first + one.shape[0]])
        first += one.shape[0]
    return (
        output,
        input_grad,
        joint_sum,
        sums[0],
        sums[1],
        projection_sum,
        sums[2],
        sums[3],
        sums[4],
        upward_sum,
        sums[5],
        downward_sum,
        sums[6],
        sums[7],
        sums[8],
    )


def solution(mesh):
    tokens = P("dp", "seq", None)
    matrix = P(EVERY, None)
    vector = P(EVERY)
    kinds = (tokens, tokens, P("dp", None), matrix, vector, vector, matrix, vector, vector, vector)
    kinds += (matrix, vector, matrix, vector, vector, vector)
    in_specs = kinds
    out_specs = kinds[:2] + kinds[3:]
    return jax.shard_map(body, mesh=mesh, in_specs=in_specs, out_specs=out_specs, check_vma=False)
```

```python
import math
from functools import partial

import jax
import jax.numpy as jnp
from jax import lax
from jax.experimental import pallas as pl
from jax.experimental.pallas import tpu as pltpu
from jax.sharding import Mesh, PartitionSpec as P

HEADS = 16
EVERY = ("seq", "z", "core")
LOG2E = math.log2(math.e)
epsilon = 1e-05
lowest = -1e30
bf16 = jnp.bfloat16
f32 = jnp.float32


def layer_norm(values, scaling, shifting):
    average = jnp.mean(values, -1, keepdims=True)
    centered = values - average
    variance = jnp.mean(centered * centered, -1, keepdims=True)
    return centered * lax.rsqrt(variance + epsilon) * scaling + shifting


def gelu_tanh(values):
    return jax.nn.gelu(values, approximate=True)


def matmul(left, right):
    return jnp.dot(left, right, preferred_element_type=f32)


def left_transposed(left, right):
    return lax.dot_general(left, right, (((0,), (0,)), ((), ())), preferred_element_type=f32)


def right_transposed(left, right):
    return lax.dot_general(left, right, (((1,), (1,)), ((), ())), preferred_element_type=f32)


def sizes():
    return lax.axis_size("seq"), lax.axis_size("z")


def places():
    return lax.axis_index("seq"), lax.axis_index("z"), lax.axis_index("core")


def to_core(value):
    return lax.ppermute(value, "core", [(0, 1), (1, 0)])


def to_seq(value, by):
    count = lax.axis_size("seq")
    return lax.ppermute(value, "seq", [(i, i ^ by) for i in range(count)])


def to_z(value, by):
    count = lax.axis_size("z")
    return lax.ppermute(value, "z", [(i, (i + by) % count) for i in range(count)])


def after(value, *others):
    return lax.optimization_barrier((value, *others))[0]


def along_z(value):
    return [value] + [to_z(value, by) for by in range(1, sizes()[1])]


def along_seq(value):
    return [value] + [to_seq(value, by) for by in range(1, sizes()[0])]


def with_core(pieces):
    return [p for piece in pieces for p in (piece, to_core(piece))]


def owner_seq_outer(nz):
    def owner(p, t, seq, z, core):
        return ((seq ^ (p // 2)) * nz + lax.rem(z - t + nz, nz)) * 2 + (core ^ (p % 2))

    return owner


def owner_z_outer(nz):
    def owner(p, t, seq, z, core):
        return ((seq ^ t) * nz + lax.rem(z - p // 2 + nz, nz)) * 2 + (core ^ (p % 2))

    return owner


def gathered_small(shard):
    ns, nz = sizes()
    seq, z, core = places()
    count = shard.shape[0]
    column = jnp.stack(along_z(shard))
    plane = jnp.stack(along_seq(column))
    both = jnp.stack([plane, to_core(plane)]).reshape(-1, count)
    device = jnp.arange(ns * nz * 2)
    s, t, c = device // (2 * nz), (device // 2) % nz, device % 2
    held_at = ((c ^ core) * ns + (s ^ seq)) * nz + (z - t + nz) % nz
    chosen = held_at[:, None] == jnp.arange(ns * nz * 2)[None]
    return matmul(chosen.astype(bf16), both)


def halves(left, right):
    ns, nz = sizes()
    tokens, depth = left.shape
    columns = right.shape[1]
    rows = depth // (ns * nz * 2)
    core = places()[2].astype(jnp.int32)
    if rows % 16:
        blocks = left_transposed(left, right).astype(bf16).reshape(ns, nz, 2, rows, columns)
        return (
            lax.dynamic_index_in_dim(blocks, core, 2, keepdims=False),
            lax.dynamic_index_in_dim(blocks, 1 - core, 2, keepdims=False),
        )
    tile = depth // ns

    def kernel(core_ref, left_ref, right_ref, mine_ref, other_ref):
        product = left_transposed(left_ref[...], right_ref[...]).astype(bf16)
        product = product.reshape(nz, 2, rows, columns)
        first = core_ref[0] == 0
        mine_ref[0] = jnp.where(first, product[:, 0], product[:, 1])
        other_ref[0] = jnp.where(first, product[:, 1], product[:, 0])

    out = pl.BlockSpec((1, nz, rows, columns), lambda i, core: (i, 0, 0, 0))
    return pl.pallas_call(
        kernel,
        name="halves",
        grid_spec=pltpu.PrefetchScalarGridSpec(
            num_scalar_prefetch=1,
            grid=(ns,),
            in_specs=[
                pl.BlockSpec((tokens, tile), lambda i, core: (0, i)),
                pl.BlockSpec((tokens, columns), lambda i, core: (0, 0)),
            ],
            out_specs=[out, out],
        ),
        out_shape=[jax.ShapeDtypeStruct((ns, nz, rows, columns), bf16)] * 2,
        compiler_params=pltpu.CompilerParams(vmem_limit_bytes=40 << 20),
        cost_estimate=pl.CostEstimate(
            flops=2 * tokens * depth * columns,
            bytes_accessed=2 * (tokens * (depth + columns) + depth * columns),
            transcendentals=0,
        ),
    )(core[None], left, right)


def joint_halves(left, rights):
    ns, nz = sizes()
    tokens, depth = left.shape
    pairs = len(rights)
    width = pairs * 128
    columns = 3 * ns * width
    rows = depth // (ns * nz * 2)
    if rows % 16:
        right = jnp.concatenate(rights, 3)
        return halves(left, right.transpose(2, 1, 0, 3).reshape(tokens, columns))
    tile = depth // ns

    def kernel(core_ref, left_ref, *refs):
        rights_ref, mine_ref, other_ref = refs[:pairs], *refs[pairs:]
        first = core_ref[0] == 0
        rows_left = left_ref[...].T
        for group in range(ns):
            for kind in range(3):
                at = (kind * ns + group) * width
                right = jnp.concatenate([ref[group, kind] for ref in rights_ref], 1)
                product = matmul(rows_left, right).astype(bf16)
                product = product.reshape(nz, 2, rows, width)
                mine_ref[0, :, :, at : at + width] = jnp.where(first, product[:, 0], product[:, 1])
                other_ref[0, :, :, at : at + width] = jnp.where(first, product[:, 1], product[:, 0])

    out = pl.BlockSpec((1, nz, rows, columns), lambda i, core: (i, 0, 0, 0))
    right = pl.BlockSpec((ns, 3, tokens, 128), lambda i, core: (0, 0, 0, 0))
    return pl.pallas_call(
        kernel,
        name="joint_halves",
        grid_spec=pltpu.PrefetchScalarGridSpec(
            num_scalar_prefetch=1,
            grid=(ns,),
            in_specs=[pl.BlockSpec((tokens, tile), lambda i, core: (0, i))] + [right] * pairs,
            out_specs=[out, out],
        ),
        out_shape=[jax.ShapeDtypeStruct((ns, nz, rows, columns), bf16)] * 2,
        compiler_params=pltpu.CompilerParams(vmem_limit_bytes=40 << 20),
        cost_estimate=pl.CostEstimate(
            flops=2 * tokens * depth * columns,
            bytes_accessed=2 * (tokens * (depth + columns) + depth * columns),
            transcendentals=0,
        ),
    )(places()[2].astype(jnp.int32)[None], left, *rights)


def joint_back(grads, weight):
    ns, _, tokens, _ = grads[0].shape
    pairs = len(grads)
    width = pairs * 128
    depth = weight.shape[0]

    def kernel(*refs):
        grads_ref, weight_ref, out_ref = refs[:pairs], *refs[pairs:]
        result = jnp.zeros((tokens, depth), f32)
        for group in range(ns):
            for kind in range(3):
                at = (kind * ns + group) * width
                grad = jnp.concatenate([ref[group, kind] for ref in grads_ref], 1)
                result += right_transposed(grad, weight_ref[:, at : at + width])
        out_ref[...] = result

    return pl.pallas_call(
        kernel,
        name="joint_back",
        out_shape=jax.ShapeDtypeStruct((tokens, depth), f32),
        compiler_params=pltpu.CompilerParams(vmem_limit_bytes=24 << 20),
        cost_estimate=pl.CostEstimate(
            flops=2 * tokens * weight.size,
            bytes_accessed=4 * weight.size + 4 * tokens * depth,
            transcendentals=0,
        ),
    )(*grads, weight)


def summed(terms, order, axis=0, cut=None):
    _, _, rows, columns = terms[0].shape
    n, m = terms[0].shape[axis], terms[0].shape[1 - axis]
    first, last = cut or (0, columns // 1024)
    count = len(terms)

    def kernel(order_ref, *refs):
        for k in range(n):
            result = refs[k * count][0, 0].astype(f32)
            for j in range(1, count):
                result = result + refs[k * count + j][0, 0].astype(f32)
            refs[n * count + k][0] = result.astype(bf16)

    def block(k):
        def index(i, c, order):
            return (order[k], i, 0, first + c) if axis == 0 else (i, order[k], 0, first + c)

        return pl.BlockSpec((1, 1, rows, 1024), index)

    size = 2 * n * m * rows * (last - first) * 1024
    return pl.pallas_call(
        kernel,
        name="summed",
        grid_spec=pltpu.PrefetchScalarGridSpec(
            num_scalar_prefetch=1,
            grid=(m, last - first),
            in_specs=[block(k) for k in range(n) for _ in range(count)],
            out_specs=[pl.BlockSpec((1, rows, 1024), lambda i, c, order: (i, 0, c))] * n,
        ),
        out_shape=[jax.ShapeDtypeStruct((m, rows, (last - first) * 1024), bf16)] * n,
        compiler_params=pltpu.CompilerParams(vmem_limit_bytes=32 << 20),
        cost_estimate=pl.CostEstimate(
            flops=0, bytes_accessed=(count + 1) * size, transcendentals=0
        ),
    )(order.astype(jnp.int32), *([*terms] * n))


def first_step(mine, other, along, cut=None):
    ns, nz = sizes()
    if mine.shape[2] % 16:
        if cut:
            mine, other = (v[..., cut[0] * 1024 : cut[1] * 1024] for v in (mine, other))
        return [(mine.astype(f32) + other.astype(f32)).astype(bf16)]
    seq, z, _ = places()
    if along == "seq":
        parts = summed([mine, other], seq ^ jnp.arange(ns), 0, cut)
        return [parts[0]] + [to_seq(parts[by], by) for by in range(1, ns)]
    parts = summed([mine, other], (z + jnp.arange(nz)) % nz, 1, cut)
    return [parts[0]] + [to_z(parts[by], by) for by in range(1, nz)]


def second_sums(terms, along):
    ns, nz = sizes()
    if len(terms) == 1:
        return terms
    seq, z, _ = places()
    order = (z + jnp.arange(nz)) % nz if along == "seq" else seq ^ jnp.arange(ns)
    return summed([term[:, None] for term in terms], order)


def second_step(parts, along):
    ns, nz = sizes()
    if len(parts) == 1:
        return parts
    if along == "seq":
        return [parts[0][0]] + [to_z(parts[by][0], by) for by in range(1, nz)]
    return [parts[0][0]] + [to_seq(parts[by][0], by) for by in range(1, ns)]


def last_step(terms):
    if len(terms) == 1:
        chip = terms[0].reshape(-1, *terms[0].shape[2:])
        return lax.psum_scatter(chip, ("seq", "z"), scatter_dimension=0, tiled=True)[0].astype(f32)
    result = terms[0].astype(f32)
    for term in terms[1:]:
        result = result + term.astype(f32)
    return result


def over_seq(value):
    return lax.all_to_all(value, "seq", 0, 0, tiled=True)


def scattered_small(values):
    ns, nz = sizes()
    seq, z, core = places()
    blocks = values.reshape(ns, nz, 2, -1)

    def pick(array, index, axis):
        return lax.dynamic_index_in_dim(array, index, axis, keepdims=False)

    chip = pick(blocks, core, 2) + to_core(pick(blocks, 1 - core, 2))
    plane = pick(chip, seq, 0)
    for by in range(1, ns):
        plane = plane + to_seq(pick(chip, seq ^ by, 0), by)
    result = pick(plane, z, 0)
    for by in range(1, nz):
        result = result + to_z(pick(plane, (z + by) % nz, 0), by)
    return result


def joint_product(normed, shard, bias, later):
    ns, nz = sizes()
    tokens, features = normed.shape
    rows, columns = shard.shape
    width = features // ns
    pairs = width // 128
    if rows % 16:
        full = lax.all_gather(shard, EVERY, axis=0, tiled=True)
        last = lax.all_gather(later, EVERY, axis=0, tiled=True)
        mixture = (matmul(normed, full) + bias).astype(bf16)
        mixture = mixture.reshape(tokens, 3, ns, pairs, 128).transpose(3, 2, 1, 0, 4)
        return full, last, [mixture[pair] for pair in range(pairs)]
    one = jnp.stack(along_z(shard))
    two = jnp.stack(along_seq(later))
    ones = with_core(along_seq(one))
    twos = with_core(along_z(two))
    owners = [owner_seq_outer(nz)] * len(ones) + [owner_z_outer(nz)] * len(twos)
    numbers = list(range(len(ones))) + list(range(len(twos)))
    pieces = ones + twos
    count = len(pieces)
    slots = sum(piece.shape[0] for piece in pieces)
    devices = slots // 2

    def kernel(place, *refs):
        ins = refs[:count]
        normed_ref, bias_ref, full_ref, last_ref = refs[count : count + 4]
        outs_ref = refs[count + 4 : count + 4 + pairs]
        held, held_last, in_sem, out_sem = refs[count + 4 + pairs :]
        copies = []
        for p in range(count):
            to = held if p < len(ones) else held_last
            for t in range(ins[p].shape[0]):
                device = owners[p](numbers[p], t, place[0], place[1], place[2])
                sem = in_sem.at[len(copies)]
                copy = pltpu.make_async_copy(ins[p].at[t], to.at[device], sem)
                copy.start()
                copies.append(copy)
        for copy in copies[:devices]:
            copy.wait()
        full_copy = pltpu.make_async_copy(held, full_ref, out_sem.at[0])
        full_copy.start()
        for kind in range(3):
            for group in range(ns):
                at = kind * features + group * width
                weight = held[:, :, at : at + width].reshape(features, width)
                product = matmul(normed_ref[...], weight) + bias_ref[:, at : at + width]
                product = product.astype(bf16)
                for pair in range(pairs):
                    outs_ref[pair][group, kind] = product[:, pair * 128 : pair * 128 + 128]
        for copy in copies[devices:]:
            copy.wait()
        last_copy = pltpu.make_async_copy(held_last, last_ref, out_sem.at[1])
        last_copy.start()
        full_copy.wait()
        last_copy.wait()

    place = jnp.stack(places()).astype(jnp.int32)
    anywhere = pl.BlockSpec(memory_space=pl.ANY)
    inside = pl.BlockSpec(memory_space=pltpu.VMEM)
    full, last, *mixture = pl.pallas_call(
        kernel,
        name="joint_product",
        out_shape=[
            jax.ShapeDtypeStruct((devices, rows, columns), bf16),
            jax.ShapeDtypeStruct((devices, *later.shape), bf16),
        ]
        + [jax.ShapeDtypeStruct((ns, 3, tokens, 128), bf16)] * pairs,
        in_specs=[pl.BlockSpec(memory_space=pltpu.SMEM)] + [anywhere] * count + [inside] * 2,
        out_specs=[anywhere, anywhere] + [inside] * pairs,
        scratch_shapes=[
            pltpu.VMEM((devices, rows, columns), bf16),
            pltpu.VMEM((devices, *later.shape), bf16),
            pltpu.SemaphoreType.DMA((slots,)),
            pltpu.SemaphoreType.DMA((2,)),
        ],
        compiler_params=pltpu.CompilerParams(vmem_limit_bytes=24 << 20),
        cost_estimate=pl.CostEstimate(
            flops=2 * tokens * features * columns,
            bytes_accessed=6 * features * columns,
            transcendentals=0,
        ),
    )(place, *pieces, normed, bias[None])
    return full.reshape(features, columns), last.reshape(features, -1), mixture


def half_lanes(shape, which):
    lane = lax.broadcasted_iota(jnp.int32, shape, len(shape) - 1)
    return (lane < 64) if which == 0 else (lane >= 64)


def with_bias(keys, slope, first_place, which):
    lane = lax.broadcasted_iota(jnp.int32, keys.shape, 1) - (64 if which == 0 else 0)
    row = lax.broadcasted_iota(jnp.int32, keys.shape, 0) + first_place
    bias = row.astype(f32) * (slope * 8.0)
    high = bias.astype(bf16)
    rest = bias - high.astype(f32)
    middle = rest.astype(bf16)
    low = (rest - middle.astype(f32)).astype(bf16)
    zero = jnp.zeros_like(high)
    terms = jnp.where(
        lane == 0, high, jnp.where(lane == 1, middle, jnp.where(lane == 2, low, zero))
    )
    return jnp.where(half_lanes(keys.shape, which), keys, terms)


def attention_forward(qkv, order, slopes):
    ns, _, length, width = qkv.shape
    pairs = width // 128
    scale = LOG2E / 8.0

    def kernel(order_ref, slope_ref, q_ref, kv_ref, low_ref, full_ref, log_ref):
        pair, place = pl.program_id(0), pl.program_id(1)
        shape = (length, 128)
        queries = [
            jnp.where(half_lanes(shape, w), q_ref[0, 0], jnp.ones(shape, bf16)) for w in (0, 1)
        ]

        def step(block, state, diagonal):
            at = order_ref[block]
            result = []
            for w in (0, 1):
                top, acc = state[w]
                keys = with_bias(kv_ref[at, 1], slope_ref[pair * 2 + w], block * length, w)
                scores = right_transposed(keys, queries[w])
                if diagonal:
                    k = lax.broadcasted_iota(jnp.int32, scores.shape, 0)
                    q = lax.broadcasted_iota(jnp.int32, scores.shape, 1)
                    scores = jnp.where(k <= q, scores, lowest)
                new_top = jnp.maximum(top, jnp.max(scores, 0, keepdims=True))
                weights = jnp.exp2(scores * scale - new_top * scale).astype(bf16)
                values = jnp.where(half_lanes(shape, w), kv_ref[at, 2], jnp.ones(shape, bf16))
                acc = acc * jnp.exp2((top - new_top) * scale) + left_transposed(values, weights)
                result.append((new_top, acc))
            return tuple(result)

        start = (jnp.full((1, length), lowest, f32), jnp.zeros((128, length), f32))
        state = lax.fori_loop(
            0, place, lambda block, state: step(block, state, False), (start, start)
        )
        (top0, acc0), (top1, acc1) = step(place, state, True)
        sum0, sum1 = acc0[64:65], acc1[0:1]
        row = lax.broadcasted_iota(jnp.int32, (128, length), 0)
        attended = jnp.where(row < 64, acc0 / sum0, acc1 / sum1).T
        full_ref[0] = attended
        low_ref[0] = attended.astype(bf16)
        row = lax.broadcasted_iota(jnp.int32, (8, length), 0)
        log_ref[0, 0] = jnp.where(
            row == 0, top0 * scale + jnp.log2(sum0), top1 * scale + jnp.log2(sum1)
        )

    per_block = 2 * 2 * length * length * 128 * 2
    grid_spec = pltpu.PrefetchScalarGridSpec(
        num_scalar_prefetch=2,
        grid=(pairs, ns),
        in_specs=[
            pl.BlockSpec((1, 1, length, 128), lambda p, i, order, slope: (order[i], 0, 0, p)),
            pl.BlockSpec((ns, 3, length, 128), lambda p, i, order, slope: (0, 0, 0, p)),
        ],
        out_specs=[
            pl.BlockSpec((1, length, 128), lambda p, i, order, slope: (order[i], 0, p)),
            pl.BlockSpec((1, length, 128), lambda p, i, order, slope: (order[i], 0, p)),
            pl.BlockSpec((1, 1, 8, length), lambda p, i, order, slope: (p, i, 0, 0)),
        ],
    )
    return pl.pallas_call(
        kernel,
        name="attention_forward",
        grid_spec=grid_spec,
        out_shape=[
            jax.ShapeDtypeStruct((ns, length, width), bf16),
            jax.ShapeDtypeStruct((ns, length, width), f32),
            jax.ShapeDtypeStruct((pairs, ns, 8, length), f32),
        ],
        compiler_params=pltpu.CompilerParams(vmem_limit_bytes=40 << 20),
        cost_estimate=pl.CostEstimate(
            flops=pairs * per_block * ns * (ns + 1) // 2 * 12,
            bytes_accessed=qkv.size * 2 + ns * length * width * 6,
            transcendentals=pairs * ns * (ns + 1) * length * length,
        ),
    )(order, slopes, qkv, qkv)


def attention_backward(qkv, grad, full, logs, order, slopes):
    ns, _, length, width = qkv.shape
    pairs = width // 128
    scale = LOG2E / 8.0

    def kernel(
        order_ref, slope_ref, qkv_ref, grad_ref, full_ref, log_ref, out_ref, dq_ref, delta_ref
    ):
        pair, block = pl.program_id(0), pl.program_id(1)
        shape = (length, 128)

        @pl.when(block == 0)
        def _():
            def one(i, _):
                at = order_ref[i]
                product = (grad_ref[at].astype(f32) * full_ref[at]).T
                delta_ref[i] = jnp.concatenate(
                    [
                        jnp.sum(product[:64], 0, keepdims=True),
                        jnp.sum(product[64:], 0, keepdims=True),
                    ],
                    0,
                )
                dq_ref[i] = jnp.zeros((128, length), f32)
                return 0

            lax.fori_loop(0, ns, one, 0)

        here = order_ref[block]
        keys, values = qkv_ref[here, 1], qkv_ref[here, 2]
        zero = jnp.zeros(shape, bf16)
        one = jnp.ones(shape, bf16)
        masks = [half_lanes(shape, w) for w in (0, 1)]
        biased = [
            with_bias(keys, slope_ref[pair * 2 + w], block * length, w) for w in (0, 1)
        ]
        own_keys = [jnp.where(masks[w], keys, zero) for w in (0, 1)]
        own_values = [jnp.where(masks[w], values, zero) for w in (0, 1)]

        def step(i, state, diagonal):
            at = order_ref[i]
            grad_keys, grad_values = state
            queries, grads = qkv_ref[at, 0], grad_ref[at]
            grad_queries = dq_ref[i]
            for w in (0, 1):
                scores = right_transposed(biased[w], jnp.where(masks[w], queries, one))
                weights = jnp.exp2(scores * scale - log_ref[0, i, w : w + 1])
                if diagonal:
                    k = lax.broadcasted_iota(jnp.int32, scores.shape, 0)
                    q = lax.broadcasted_iota(jnp.int32, scores.shape, 1)
                    weights = jnp.where(k <= q, weights, 0.0)
                grad_weights = right_transposed(own_values[w], grads)
                grad_scores = (weights * (grad_weights - delta_ref[i, w : w + 1])).astype(bf16)
                own_grads = jnp.where(masks[w], grads, zero)
                own_queries = jnp.where(masks[w], queries, zero)
                grad_values = grad_values + matmul(weights.astype(bf16), own_grads)
                grad_keys = grad_keys + matmul(grad_scores, own_queries)
                grad_queries = grad_queries + left_transposed(own_keys[w], grad_scores)
            dq_ref[i] = grad_queries
            return grad_keys, grad_values

        start = (jnp.zeros(shape, f32), jnp.zeros(shape, f32))
        state = step(block, start, True)
        grad_keys, grad_values = lax.fori_loop(
            block + 1, ns, lambda i, state: step(i, state, False), state
        )
        out_ref[here, 1] = (grad_keys * 0.125).astype(bf16)
        out_ref[here, 2] = grad_values.astype(bf16)
        out_ref[here, 0] = (dq_ref[block].T * 0.125).astype(bf16)

    per_block = 2 * 5 * length * length * 128 * 2
    grid_spec = pltpu.PrefetchScalarGridSpec(
        num_scalar_prefetch=2,
        grid=(pairs, ns),
        in_specs=[
            pl.BlockSpec((ns, 3, length, 128), lambda p, i, order, slope: (0, 0, 0, p)),
            pl.BlockSpec((ns, length, 128), lambda p, i, order, slope: (0, 0, p)),
            pl.BlockSpec((ns, length, 128), lambda p, i, order, slope: (0, 0, p)),
            pl.BlockSpec((1, ns, 8, length), lambda p, i, order, slope: (p, 0, 0, 0)),
        ],
        out_specs=pl.BlockSpec((ns, 3, length, 128), lambda p, i, order, slope: (0, 0, 0, p)),
        scratch_shapes=[
            pltpu.VMEM((ns, 128, length), f32),
            pltpu.VMEM((ns, 2, length), f32),
        ],
    )
    return pl.pallas_call(
        kernel,
        name="attention_backward",
        grid_spec=grid_spec,
        out_shape=jax.ShapeDtypeStruct((ns, 3, length, width), bf16),
        compiler_params=pltpu.CompilerParams(vmem_limit_bytes=48 << 20),
        cost_estimate=pl.CostEstimate(
            flops=pairs * per_block * ns * (ns + 1) // 2 * 12,
            bytes_accessed=qkv.size * 4 + ns * length * width * 6,
            transcendentals=pairs * ns * (ns + 1) * length * length,
        ),
    )(order, slopes, qkv, grad, full, logs)


def body(
    tokens,
    cotangent,
    block_order,
    joint_weight,
    query_bias,
    value_bias,
    projection,
    offset,
    first_gain,
    first_shift,
    upward_weight,
    upward_bias,
    downward_weight,
    downward_bias,
    second_gain,
    second_shift,
):
    members, length, features = tokens.shape
    ns, nz = sizes()
    seq = lax.axis_index("seq")
    width = features // ns
    group = HEADS // ns
    devices = ns * nz * 2

    small = (
        query_bias,
        value_bias,
        offset,
        first_gain,
        first_shift,
        upward_bias,
        downward_bias,
        second_gain,
        second_shift,
    )
    sizes_small = [one.shape[0] for one in small]
    count = sum(sizes_small)
    packed, first = jnp.zeros((count,), f32), 0
    for one in small:
        packed += jnp.pad(one.astype(f32), (first, count - first - one.shape[0]))
        first += one.shape[0]
    packed = gathered_small(packed.astype(bf16))
    smalls, first = [], 0
    for one in small:
        smalls.append(packed[:, first : first + one.shape[0]].reshape(-1))
        first += one.shape[0]
    (
        query_add,
        value_add,
        offset_add,
        gain_one,
        shift_one,
        upward_add,
        downward_add,
        gain_two,
        shift_two,
    ) = smalls

    upward_full = lax.all_gather(upward_weight, EVERY, axis=0, tiled=True)
    downward_full = lax.all_gather(downward_weight, EVERY, axis=0, tiled=True)

    slopes = 2.0 ** (-8.0 * (jnp.arange(HEADS, dtype=f32) + 1.0) / HEADS) * (4.0 / (length * ns))
    slopes = lax.dynamic_slice_in_dim(slopes, seq * group, group)
    order = jnp.argsort(block_order[0]).astype(jnp.int32)

    inputs = tokens.reshape(length, features).astype(f32)
    normed, first_pull = jax.vjp(layer_norm, inputs, gain_one, shift_one)
    normed_low = normed.astype(bf16)
    zeros = jnp.zeros_like(query_add)
    bias = jnp.concatenate([query_add, zeros, value_add])
    joint_full, projection_full, mixture = joint_product(
        normed_low, joint_weight, bias, projection
    )
    pairs = len(mixture)
    slopes = slopes.reshape(pairs, 2)
    qkv = [over_seq(one) for one in mixture]
    forward = [attention_forward(qkv[pair], order, slopes[pair]) for pair in range(pairs)]
    attended = jnp.stack([over_seq(one[0]) for one in forward])
    attended_low = attended.transpose(2, 1, 0, 3).reshape(length, features)

    middle = inputs + matmul(attended_low, projection_full) + offset_add
    second, second_pull = jax.vjp(layer_norm, middle, gain_two, shift_two)
    second_low = second.astype(bf16)
    hidden = matmul(second_low, upward_full) + upward_add
    active, gelu_pull = jax.vjp(gelu_tanh, hidden)
    active_low = active.astype(bf16)
    result = matmul(active_low, downward_full) + downward_add
    output = (middle + result).astype(bf16).reshape(members, length, features)

    grad_result = cotangent.reshape(length, features)
    grad_result_full = grad_result.astype(f32)
    downward_mine, downward_other = halves(active_low, grad_result)
    downwardbias_grad = jnp.sum(grad_result_full, 0)
    downward_other = to_core(downward_other)
    (grad_hidden,) = gelu_pull(right_transposed(after(grad_result, downward_mine), downward_full))
    grad_hidden_low = grad_hidden.astype(bf16)
    downward_chip = (downward_mine.astype(f32) + downward_other.astype(f32)).astype(bf16)
    downward_sum = lax.psum_scatter(
        downward_chip.reshape(ns * nz, -1, features), ("seq", "z"), scatter_dimension=0, tiled=True
    )[0].astype(f32)
    upward_mine, upward_other = halves(after(second_low, downward_chip), grad_hidden_low)
    upward_other = to_core(upward_other)
    upwardbias_grad = jnp.sum(grad_hidden_low.astype(f32), 0)
    grad_second = right_transposed(after(grad_hidden_low, upward_mine), upward_full)
    middle_part, secondgain_grad, secondshift_grad = second_pull(grad_second)

    grad_middle = grad_result_full + middle_part
    grad_branch = grad_middle.astype(bf16)
    offset_grad = jnp.sum(grad_branch.astype(f32), 0)
    grad_attended = right_transposed(grad_branch, projection_full).astype(bf16)
    grad_attended = grad_attended.reshape(length, ns, pairs, 128).transpose(2, 1, 0, 3)
    grad_attended = [over_seq(grad_attended[pair]) for pair in range(pairs)]
    projection_mine, projection_other = halves(attended_low, grad_branch)
    projection_other = to_core(projection_other)
    upward_terms = first_step(upward_mine, upward_other, "seq")
    projection_terms = first_step(projection_mine, projection_other, "seq")
    grad_attended[0] = after(grad_attended[0], upward_terms[0], projection_terms[0])
    grad_qkv = []
    for pair in range(pairs):
        if pair == pairs - 1:
            upward_parts = second_sums(upward_terms, "seq")
            projection_parts = second_sums(projection_terms, "seq")
            grad_attended[pair] = after(grad_attended[pair], upward_parts[0], projection_parts[0])
        low, full, logs = forward[pair]
        grad = attention_backward(qkv[pair], grad_attended[pair], full, logs, order, slopes[pair])
        grad_qkv.append(over_seq(grad))
    upward_sum = last_step(second_step(upward_parts, "seq"))
    projection_sum = last_step(second_step(projection_parts, "seq"))
    grad_qkv[0] = after(grad_qkv[0], upward_sum, projection_sum, downward_sum, output)
    joint_mine, joint_other = joint_halves(normed_low, grad_qkv)
    joint_other = to_core(joint_other)
    joint_terms = first_step(joint_mine, joint_other, "seq", (0, 2))
    joint_more = first_step(joint_mine, joint_other, "z", (2, 3))
    joint_parts = second_sums(joint_terms, "seq")
    more_parts = second_sums(joint_more, "z")
    joint_terms = second_step(joint_parts, "seq")
    joint_more = second_step(more_parts, "z")
    joint_sum = jnp.concatenate([last_step(joint_terms), last_step(joint_more)], 1)
    grad_qkv[0] = after(grad_qkv[0], joint_parts[0], more_parts[0])
    mixture_sums = jnp.stack([jnp.sum(grad.astype(f32), 2) for grad in grad_qkv])
    mixture_sums = mixture_sums.transpose(2, 1, 0, 3).reshape(-1)
    grad_normed = joint_back(grad_qkv, joint_full)
    input_part, firstgain_grad, firstshift_grad = first_pull(grad_normed)
    input_grad = (grad_middle + input_part).astype(bf16).reshape(members, length, features)

    grads = (
        mixture_sums[:features],
        mixture_sums[2 * features :],
        offset_grad,
        firstgain_grad,
        firstshift_grad,
        upwardbias_grad,
        downwardbias_grad,
        secondgain_grad,
        secondshift_grad,
    )
    packed = jnp.concatenate([g.reshape(devices, -1) for g in grads], 1)
    packed = scattered_small(packed)
    sums, first = [], 0
    for one in small:
        sums.append(packed[first : first + one.shape[0]])
        first += one.shape[0]
    return (
        output,
        input_grad,
        joint_sum,
        sums[0],
        sums[1],
        projection_sum,
        sums[2],
        sums[3],
        sums[4],
        upward_sum,
        sums[5],
        downward_sum,
        sums[6],
        sums[7],
        sums[8],
    )


def solution(mesh):
    ns, dp = mesh.devices.shape
    split = Mesh(mesh.devices.reshape(ns, dp // 2, 2), EVERY)
    tokens = P(("z", "core"), "seq", None)
    matrix = P(EVERY, None)
    vector = P(EVERY)
    orders = P(("z", "core"), None)
    kinds = (tokens, tokens, orders, matrix, vector, vector, matrix, vector, vector, vector)
    kinds += (matrix, vector, matrix, vector, vector, vector)
    in_specs = kinds
    out_specs = kinds[:2] + kinds[3:]
    return jax.shard_map(body, mesh=split, in_specs=in_specs, out_specs=out_specs, check_vma=False)
```

```python
import math
from functools import partial

import jax
import jax.numpy as jnp
from jax import lax
from jax.experimental import pallas as pl
from jax.experimental.pallas import tpu as pltpu
from jax.sharding import Mesh, PartitionSpec as P

HEADS = 16
EVERY = ("seq", "z", "core")
LOG2E = math.log2(math.e)
epsilon = 1e-05
lowest = -1e30
bf16 = jnp.bfloat16
f32 = jnp.float32


def layer_norm(values, scaling, shifting):
    average = jnp.mean(values, -1, keepdims=True)
    centered = values - average
    variance = jnp.mean(centered * centered, -1, keepdims=True)
    return centered * lax.rsqrt(variance + epsilon) * scaling + shifting


def gelu_both(values):
    slope = math.sqrt(2.0 / math.pi)
    square = values * values
    curve = jnp.tanh(slope * values * (1.0 + 0.044715 * square))
    half = 0.5 * (1.0 + curve)
    inner = slope * (1.0 + 3 * 0.044715 * square)
    return values * half, half + 0.5 * values * (1.0 - curve * curve) * inner


def matmul(left, right):
    return jnp.dot(left, right, preferred_element_type=f32)


def left_transposed(left, right):
    return lax.dot_general(left, right, (((0,), (0,)), ((), ())), preferred_element_type=f32)


def right_transposed(left, right):
    return lax.dot_general(left, right, (((1,), (1,)), ((), ())), preferred_element_type=f32)


def sizes():
    return lax.axis_size("seq"), lax.axis_size("z")


def places():
    return lax.axis_index("seq"), lax.axis_index("z"), lax.axis_index("core")


def to_core(value):
    return lax.ppermute(value, "core", [(0, 1), (1, 0)])


def to_seq(value, by):
    count = lax.axis_size("seq")
    return lax.ppermute(value, "seq", [(i, i ^ by) for i in range(count)])


def to_z(value, by):
    count = lax.axis_size("z")
    return lax.ppermute(value, "z", [(i, (i + by) % count) for i in range(count)])


def after(value, *others):
    return lax.optimization_barrier((value, *others))[0]


def along_z(value):
    return [value] + [to_z(value, by) for by in range(1, sizes()[1])]


def along_seq(value):
    return [value] + [to_seq(value, by) for by in range(1, sizes()[0])]


def with_core(pieces):
    return [p for piece in pieces for p in (piece, to_core(piece))]


def owner_seq_outer(nz):
    def owner(p, t, seq, z, core):
        return ((seq ^ (p // 2)) * nz + lax.rem(z - t + nz, nz)) * 2 + (core ^ (p % 2))

    return owner


def owner_z_outer(nz):
    def owner(p, t, seq, z, core):
        return ((seq ^ t) * nz + lax.rem(z - p // 2 + nz, nz)) * 2 + (core ^ (p % 2))

    return owner


def gathered_small(shard):
    ns, nz = sizes()
    seq, z, core = places()
    count = shard.shape[0]
    column = jnp.stack(along_z(shard))
    plane = jnp.stack(along_seq(column))
    both = jnp.stack([plane, to_core(plane)]).reshape(-1, count)
    device = jnp.arange(ns * nz * 2)
    s, t, c = device // (2 * nz), (device // 2) % nz, device % 2
    held_at = ((c ^ core) * ns + (s ^ seq)) * nz + (z - t + nz) % nz
    chosen = held_at[:, None] == jnp.arange(ns * nz * 2)[None]
    return matmul(chosen.astype(bf16), both)


def halves(left, right):
    ns, nz = sizes()
    tokens, depth = left.shape
    columns = right.shape[1]
    rows = depth // (ns * nz * 2)
    core = places()[2].astype(jnp.int32)
    if rows % 16:
        blocks = left_transposed(left, right).astype(bf16).reshape(ns, nz, 2, rows, columns)
        return (
            lax.dynamic_index_in_dim(blocks, core, 2, keepdims=False),
            lax.dynamic_index_in_dim(blocks, 1 - core, 2, keepdims=False),
        )
    tile = depth // ns

    def kernel(core_ref, left_ref, right_ref, mine_ref, other_ref):
        product = left_transposed(left_ref[...], right_ref[...]).astype(bf16)
        product = product.reshape(nz, 2, rows, columns)
        first = core_ref[0] == 0
        mine_ref[0] = jnp.where(first, product[:, 0], product[:, 1])
        other_ref[0] = jnp.where(first, product[:, 1], product[:, 0])

    out = pl.BlockSpec((1, nz, rows, columns), lambda i, core: (i, 0, 0, 0))
    return pl.pallas_call(
        kernel,
        name="halves",
        grid_spec=pltpu.PrefetchScalarGridSpec(
            num_scalar_prefetch=1,
            grid=(ns,),
            in_specs=[
                pl.BlockSpec((tokens, tile), lambda i, core: (0, i)),
                pl.BlockSpec((tokens, columns), lambda i, core: (0, 0)),
            ],
            out_specs=[out, out],
        ),
        out_shape=[jax.ShapeDtypeStruct((ns, nz, rows, columns), bf16)] * 2,
        compiler_params=pltpu.CompilerParams(vmem_limit_bytes=40 << 20),
        cost_estimate=pl.CostEstimate(
            flops=2 * tokens * depth * columns,
            bytes_accessed=2 * (tokens * (depth + columns) + depth * columns),
            transcendentals=0,
        ),
    )(core[None], left, right)


def joint_halves(left, rights):
    ns, nz = sizes()
    tokens, depth = left.shape
    pairs = len(rights)
    width = pairs * 128
    columns = 3 * ns * width
    rows = depth // (ns * nz * 2)
    if rows % 16:
        right = jnp.concatenate(rights, 3)
        return halves(left, right.transpose(2, 1, 0, 3).reshape(tokens, columns))
    tile = depth // ns

    def kernel(core_ref, left_ref, *refs):
        rights_ref, mine_ref, other_ref = refs[:pairs], *refs[pairs:]
        first = core_ref[0] == 0
        rows_left = left_ref[...].T
        for group in range(ns):
            for kind in range(3):
                at = (kind * ns + group) * width
                right = jnp.concatenate([ref[group, kind] for ref in rights_ref], 1)
                product = matmul(rows_left, right).astype(bf16)
                product = product.reshape(nz, 2, rows, width)
                mine_ref[0, :, :, at : at + width] = jnp.where(first, product[:, 0], product[:, 1])
                other_ref[0, :, :, at : at + width] = jnp.where(first, product[:, 1], product[:, 0])

    out = pl.BlockSpec((1, nz, rows, columns), lambda i, core: (i, 0, 0, 0))
    right = pl.BlockSpec((ns, 3, tokens, 128), lambda i, core: (0, 0, 0, 0))
    return pl.pallas_call(
        kernel,
        name="joint_halves",
        grid_spec=pltpu.PrefetchScalarGridSpec(
            num_scalar_prefetch=1,
            grid=(ns,),
            in_specs=[pl.BlockSpec((tokens, tile), lambda i, core: (0, i))] + [right] * pairs,
            out_specs=[out, out],
        ),
        out_shape=[jax.ShapeDtypeStruct((ns, nz, rows, columns), bf16)] * 2,
        compiler_params=pltpu.CompilerParams(vmem_limit_bytes=40 << 20),
        cost_estimate=pl.CostEstimate(
            flops=2 * tokens * depth * columns,
            bytes_accessed=2 * (tokens * (depth + columns) + depth * columns),
            transcendentals=0,
        ),
    )(places()[2].astype(jnp.int32)[None], left, *rights)


def joint_back(grads, weight):
    ns, _, tokens, _ = grads[0].shape
    pairs = len(grads)
    width = pairs * 128
    depth = weight.shape[0]

    def kernel(*refs):
        grads_ref, weight_ref, out_ref = refs[:pairs], *refs[pairs:]
        result = jnp.zeros((tokens, depth), f32)
        for group in range(ns):
            for kind in range(3):
                at = (kind * ns + group) * width
                grad = jnp.concatenate([ref[group, kind] for ref in grads_ref], 1)
                result += right_transposed(grad, weight_ref[:, at : at + width])
        out_ref[...] = result

    return pl.pallas_call(
        kernel,
        name="joint_back",
        out_shape=jax.ShapeDtypeStruct((tokens, depth), f32),
        compiler_params=pltpu.CompilerParams(vmem_limit_bytes=24 << 20),
        cost_estimate=pl.CostEstimate(flops=0, bytes_accessed=depth, transcendentals=0),
    )(*grads, weight)


def summed(terms, order, extra=()):
    n, m, rows, columns = terms[0].shape
    more = extra[0].shape[3] if extra else 0
    count, both = len(terms), len(terms) + len(extra)

    def kernel(order_ref, *refs):
        for k in range(n):
            ins, out = refs[k * both : (k + 1) * both], refs[n * both + k]
            for group, start, size in ((ins[:count], 0, columns), (ins[count:], columns, more)):
                if size:
                    result = group[0][0, 0].astype(f32)
                    for ref in group[1:]:
                        result = result + ref[0, 0].astype(f32)
                    out[0, :, start : start + size] = result.astype(bf16)

    def block(k, size):
        return pl.BlockSpec((1, 1, rows, size), lambda i, order: (order[k], i, 0, 0))

    in_specs = []
    for k in range(n):
        in_specs += [block(k, columns)] * count + [block(k, more)] * len(extra)
    total = columns + more
    return pl.pallas_call(
        kernel,
        name="summed",
        grid_spec=pltpu.PrefetchScalarGridSpec(
            num_scalar_prefetch=1,
            grid=(m,),
            in_specs=in_specs,
            out_specs=[pl.BlockSpec((1, rows, total), lambda i, order: (i, 0, 0))] * n,
        ),
        out_shape=[jax.ShapeDtypeStruct((m, rows, total), bf16)] * n,
        compiler_params=pltpu.CompilerParams(vmem_limit_bytes=32 << 20),
        cost_estimate=pl.CostEstimate(
            flops=0, bytes_accessed=(count + 1) * 2 * n * m * rows * total, transcendentals=0
        ),
    )(order.astype(jnp.int32), *([*terms, *extra] * n))


def seq_step(mine, other, extra=()):
    ns = sizes()[0]
    if mine.shape[2] % 16:
        chip = mine.astype(f32) + other.astype(f32)
        if extra:
            chip = jnp.concatenate([chip, extra[0].astype(f32) + extra[1].astype(f32)], 3)
        return [chip.astype(bf16)]
    parts = summed([mine, other], places()[0] ^ jnp.arange(ns), extra)
    return [parts[0]] + [to_seq(parts[by], by) for by in range(1, ns)]


def column_sums(terms):
    if len(terms) == 1:
        return terms
    nz = sizes()[1]
    return summed([term[:, None] for term in terms], (places()[1] + jnp.arange(nz)) % nz)


def z_step(parts):
    if len(parts) == 1:
        return parts
    return [parts[0][0]] + [to_z(parts[by][0], by) for by in range(1, sizes()[1])]


def last_step(terms):
    if len(terms) == 1:
        chip = terms[0].reshape(-1, *terms[0].shape[2:])
        return lax.psum_scatter(chip, ("seq", "z"), scatter_dimension=0, tiled=True)[0].astype(f32)
    result = terms[0].astype(f32)
    for term in terms[1:]:
        result = result + term.astype(f32)
    return result


def over_seq(value):
    return lax.all_to_all(value, "seq", 0, 0, tiled=True)


def scattered_small(values):
    ns, nz = sizes()
    seq, z, core = places()
    blocks = values.reshape(ns, nz, 2, -1)

    def pick(array, index, axis):
        return lax.dynamic_index_in_dim(array, index, axis, keepdims=False)

    chip = pick(blocks, core, 2) + to_core(pick(blocks, 1 - core, 2))
    plane = pick(chip, seq, 0)
    for by in range(1, ns):
        plane = plane + to_seq(pick(chip, seq ^ by, 0), by)
    result = pick(plane, z, 0)
    for by in range(1, nz):
        result = result + to_z(pick(plane, (z + by) % nz, 0), by)
    return result


def joint_product(normed, shard, bias, later):
    ns, nz = sizes()
    tokens, features = normed.shape
    rows, columns = shard.shape
    width = features // ns
    pairs = width // 128
    if rows % 16:
        full = lax.all_gather(shard, EVERY, axis=0, tiled=True)
        last = lax.all_gather(later, EVERY, axis=0, tiled=True)
        mixture = (matmul(normed, full) + bias).astype(bf16)
        mixture = mixture.reshape(tokens, 3, ns, pairs, 128).transpose(3, 2, 1, 0, 4)
        return full, last, [mixture[pair] for pair in range(pairs)]
    one = jnp.stack(along_z(shard))
    two = after(jnp.stack(along_seq(later)), one)
    ones = with_core(along_seq(one))
    twos = with_core(along_z(two))
    owners = [owner_seq_outer(nz)] * len(ones) + [owner_z_outer(nz)] * len(twos)
    numbers = list(range(len(ones))) + list(range(len(twos)))
    pieces = ones + twos
    count = len(pieces)
    slots = sum(piece.shape[0] for piece in pieces)
    devices = slots // 2

    def kernel(place, *refs):
        ins = refs[:count]
        normed_ref, bias_ref, full_ref, last_ref = refs[count : count + 4]
        outs_ref = refs[count + 4 : count + 4 + pairs]
        held, held_last, in_sem, out_sem = refs[count + 4 + pairs :]
        copies = []
        for p in range(count):
            to = held if p < len(ones) else held_last
            for t in range(ins[p].shape[0]):
                device = owners[p](numbers[p], t, place[0], place[1], place[2])
                sem = in_sem.at[len(copies)]
                copy = pltpu.make_async_copy(ins[p].at[t], to.at[device], sem)
                copy.start()
                copies.append(copy)
        for copy in copies[:devices]:
            copy.wait()
        full_copy = pltpu.make_async_copy(held, full_ref, out_sem.at[0])
        full_copy.start()
        for kind in range(3):
            for group in range(ns):
                at = kind * features + group * width
                weight = held[:, :, at : at + width].reshape(features, width)
                product = matmul(normed_ref[...], weight) + bias_ref[:, at : at + width]
                product = product.astype(bf16)
                for pair in range(pairs):
                    outs_ref[pair][group, kind] = product[:, pair * 128 : pair * 128 + 128]
        for copy in copies[devices:]:
            copy.wait()
        last_copy = pltpu.make_async_copy(held_last, last_ref, out_sem.at[1])
        last_copy.start()
        full_copy.wait()
        last_copy.wait()

    place = jnp.stack(places()).astype(jnp.int32)
    anywhere = pl.BlockSpec(memory_space=pl.ANY)
    inside = pl.BlockSpec(memory_space=pltpu.VMEM)
    full, last, *mixture = pl.pallas_call(
        kernel,
        name="joint_product",
        out_shape=[
            jax.ShapeDtypeStruct((devices, rows, columns), bf16),
            jax.ShapeDtypeStruct((devices, *later.shape), bf16),
        ]
        + [jax.ShapeDtypeStruct((ns, 3, tokens, 128), bf16)] * pairs,
        in_specs=[pl.BlockSpec(memory_space=pltpu.SMEM)] + [anywhere] * count + [inside] * 2,
        out_specs=[anywhere, anywhere] + [inside] * pairs,
        scratch_shapes=[
            pltpu.VMEM((devices, rows, columns), bf16),
            pltpu.VMEM((devices, *later.shape), bf16),
            pltpu.SemaphoreType.DMA((slots,)),
            pltpu.SemaphoreType.DMA((2,)),
        ],
        compiler_params=pltpu.CompilerParams(vmem_limit_bytes=24 << 20),
        cost_estimate=pl.CostEstimate(
            flops=2 * tokens * features * columns,
            bytes_accessed=6 * features * columns,
            transcendentals=0,
        ),
    )(place, *pieces, normed, bias[None])
    return full.reshape(features, columns), last.reshape(features, -1), mixture


def half_lanes(shape, which):
    lane = lax.broadcasted_iota(jnp.int32, shape, len(shape) - 1)
    return (lane < 64) if which == 0 else (lane >= 64)


def with_bias(keys, slope, first_place, which):
    lane = lax.broadcasted_iota(jnp.int32, keys.shape, 1) - (64 if which == 0 else 0)
    row = lax.broadcasted_iota(jnp.int32, keys.shape, 0) + first_place
    bias = row.astype(f32) * (slope * 8.0)
    high = bias.astype(bf16)
    rest = bias - high.astype(f32)
    middle = rest.astype(bf16)
    low = (rest - middle.astype(f32)).astype(bf16)
    zero = jnp.zeros_like(high)
    terms = jnp.where(
        lane == 0, high, jnp.where(lane == 1, middle, jnp.where(lane == 2, low, zero))
    )
    return jnp.where(half_lanes(keys.shape, which), keys, terms)


def attention_forward(qkv, order, slopes):
    ns, _, length, width = qkv.shape
    pairs = width // 128
    scale = LOG2E / 8.0

    def kernel(order_ref, slope_ref, q_ref, kv_ref, low_ref, full_ref, log_ref):
        pair, place = pl.program_id(0), pl.program_id(1)
        shape = (length, 128)
        queries = [
            jnp.where(half_lanes(shape, w), q_ref[0, 0], jnp.ones(shape, bf16)) for w in (0, 1)
        ]

        def step(block, state, diagonal):
            at = order_ref[block]
            result = []
            for w in (0, 1):
                top, acc = state[w]
                keys = with_bias(kv_ref[at, 1], slope_ref[pair * 2 + w], block * length, w)
                scores = right_transposed(keys, queries[w])
                if diagonal:
                    k = lax.broadcasted_iota(jnp.int32, scores.shape, 0)
                    q = lax.broadcasted_iota(jnp.int32, scores.shape, 1)
                    scores = jnp.where(k <= q, scores, lowest)
                new_top = jnp.maximum(top, jnp.max(scores, 0, keepdims=True))
                weights = jnp.exp2(scores * scale - new_top * scale).astype(bf16)
                values = jnp.where(half_lanes(shape, w), kv_ref[at, 2], jnp.ones(shape, bf16))
                acc = acc * jnp.exp2((top - new_top) * scale) + left_transposed(values, weights)
                result.append((new_top, acc))
            return tuple(result)

        start = (jnp.full((1, length), lowest, f32), jnp.zeros((128, length), f32))
        state = lax.fori_loop(
            0, place, lambda block, state: step(block, state, False), (start, start)
        )
        (top0, acc0), (top1, acc1) = step(place, state, True)
        sum0, sum1 = acc0[64:65], acc1[0:1]
        row = lax.broadcasted_iota(jnp.int32, (128, length), 0)
        attended = jnp.where(row < 64, acc0 / sum0, acc1 / sum1).T
        full_ref[0] = attended
        low_ref[0] = attended.astype(bf16)
        row = lax.broadcasted_iota(jnp.int32, (8, length), 0)
        log_ref[0, 0] = jnp.where(
            row == 0, top0 * scale + jnp.log2(sum0), top1 * scale + jnp.log2(sum1)
        )

    per_block = 2 * 2 * length * length * 128 * 2
    grid_spec = pltpu.PrefetchScalarGridSpec(
        num_scalar_prefetch=2,
        grid=(pairs, ns),
        in_specs=[
            pl.BlockSpec((1, 1, length, 128), lambda p, i, order, slope: (order[i], 0, 0, p)),
            pl.BlockSpec((ns, 3, length, 128), lambda p, i, order, slope: (0, 0, 0, p)),
        ],
        out_specs=[
            pl.BlockSpec((1, length, 128), lambda p, i, order, slope: (order[i], 0, p)),
            pl.BlockSpec((1, length, 128), lambda p, i, order, slope: (order[i], 0, p)),
            pl.BlockSpec((1, 1, 8, length), lambda p, i, order, slope: (p, i, 0, 0)),
        ],
    )
    return pl.pallas_call(
        kernel,
        name="attention_forward",
        grid_spec=grid_spec,
        out_shape=[
            jax.ShapeDtypeStruct((ns, length, width), bf16),
            jax.ShapeDtypeStruct((ns, length, width), f32),
            jax.ShapeDtypeStruct((pairs, ns, 8, length), f32),
        ],
        compiler_params=pltpu.CompilerParams(vmem_limit_bytes=40 << 20),
        cost_estimate=pl.CostEstimate(
            flops=pairs * per_block * ns * (ns + 1) // 2 * 12,
            bytes_accessed=qkv.size * 2 + ns * length * width * 6,
            transcendentals=pairs * ns * (ns + 1) * length * length,
        ),
    )(order, slopes, qkv, qkv)


def attention_backward(qkv, grad, full, logs, order, slopes):
    ns, _, length, width = qkv.shape
    pairs = width // 128
    scale = LOG2E / 8.0

    def kernel(
        order_ref, slope_ref, qkv_ref, grad_ref, full_ref, log_ref, out_ref, dq_ref, delta_ref
    ):
        pair, block = pl.program_id(0), pl.program_id(1)
        shape = (length, 128)

        @pl.when(block == 0)
        def _():
            def one(i, _):
                at = order_ref[i]
                product = (grad_ref[at].astype(f32) * full_ref[at]).T
                delta_ref[i] = jnp.concatenate(
                    [
                        jnp.sum(product[:64], 0, keepdims=True),
                        jnp.sum(product[64:], 0, keepdims=True),
                    ],
                    0,
                )
                dq_ref[i] = jnp.zeros((128, length), f32)
                return 0

            lax.fori_loop(0, ns, one, 0)

        here = order_ref[block]
        keys, values = qkv_ref[here, 1], qkv_ref[here, 2]
        zero = jnp.zeros(shape, bf16)
        one = jnp.ones(shape, bf16)
        masks = [half_lanes(shape, w) for w in (0, 1)]
        biased = [
            with_bias(keys, slope_ref[pair * 2 + w], block * length, w) for w in (0, 1)
        ]
        own_keys = [jnp.where(masks[w], keys, zero) for w in (0, 1)]
        own_values = [jnp.where(masks[w], values, zero) for w in (0, 1)]

        def step(i, state, diagonal):
            at = order_ref[i]
            grad_keys, grad_values = state
            queries, grads = qkv_ref[at, 0], grad_ref[at]
            grad_queries = dq_ref[i]
            for w in (0, 1):
                scores = right_transposed(biased[w], jnp.where(masks[w], queries, one))
                weights = jnp.exp2(scores * scale - log_ref[0, i, w : w + 1])
                if diagonal:
                    k = lax.broadcasted_iota(jnp.int32, scores.shape, 0)
                    q = lax.broadcasted_iota(jnp.int32, scores.shape, 1)
                    weights = jnp.where(k <= q, weights, 0.0)
                grad_weights = right_transposed(own_values[w], grads)
                grad_scores = (weights * (grad_weights - delta_ref[i, w : w + 1])).astype(bf16)
                own_grads = jnp.where(masks[w], grads, zero)
                own_queries = jnp.where(masks[w], queries, zero)
                grad_values = grad_values + matmul(weights.astype(bf16), own_grads)
                grad_keys = grad_keys + matmul(grad_scores, own_queries)
                grad_queries = grad_queries + left_transposed(own_keys[w], grad_scores)
            dq_ref[i] = grad_queries
            return grad_keys, grad_values

        start = (jnp.zeros(shape, f32), jnp.zeros(shape, f32))
        state = step(block, start, True)
        grad_keys, grad_values = lax.fori_loop(
            block + 1, ns, lambda i, state: step(i, state, False), state
        )
        out_ref[here, 1] = (grad_keys * 0.125).astype(bf16)
        out_ref[here, 2] = grad_values.astype(bf16)
        out_ref[here, 0] = (dq_ref[block].T * 0.125).astype(bf16)

    per_block = 2 * 5 * length * length * 128 * 2
    grid_spec = pltpu.PrefetchScalarGridSpec(
        num_scalar_prefetch=2,
        grid=(pairs, ns),
        in_specs=[
            pl.BlockSpec((ns, 3, length, 128), lambda p, i, order, slope: (0, 0, 0, p)),
            pl.BlockSpec((ns, length, 128), lambda p, i, order, slope: (0, 0, p)),
            pl.BlockSpec((ns, length, 128), lambda p, i, order, slope: (0, 0, p)),
            pl.BlockSpec((1, ns, 8, length), lambda p, i, order, slope: (p, 0, 0, 0)),
        ],
        out_specs=pl.BlockSpec((ns, 3, length, 128), lambda p, i, order, slope: (0, 0, 0, p)),
        scratch_shapes=[
            pltpu.VMEM((ns, 128, length), f32),
            pltpu.VMEM((ns, 2, length), f32),
        ],
    )
    return pl.pallas_call(
        kernel,
        name="attention_backward",
        grid_spec=grid_spec,
        out_shape=jax.ShapeDtypeStruct((ns, 3, length, width), bf16),
        compiler_params=pltpu.CompilerParams(vmem_limit_bytes=48 << 20),
        cost_estimate=pl.CostEstimate(
            flops=pairs * per_block * ns * (ns + 1) // 2 * 12,
            bytes_accessed=qkv.size * 4 + ns * length * width * 6,
            transcendentals=pairs * ns * (ns + 1) * length * length,
        ),
    )(order, slopes, qkv, grad, full, logs)


def body(
    tokens,
    cotangent,
    block_order,
    joint_weight,
    query_bias,
    value_bias,
    projection,
    offset,
    first_gain,
    first_shift,
    upward_weight,
    upward_bias,
    downward_weight,
    downward_bias,
    second_gain,
    second_shift,
):
    members, length, features = tokens.shape
    ns, nz = sizes()
    seq = lax.axis_index("seq")
    width = features // ns
    group = HEADS // ns
    devices = ns * nz * 2

    small = (
        query_bias,
        value_bias,
        offset,
        first_gain,
        first_shift,
        upward_bias,
        downward_bias,
        second_gain,
        second_shift,
    )
    sizes_small = [one.shape[0] for one in small]
    count = sum(sizes_small)
    packed, first = jnp.zeros((count,), f32), 0
    for one in small:
        packed += jnp.pad(one.astype(f32), (first, count - first - one.shape[0]))
        first += one.shape[0]
    packed = gathered_small(packed.astype(bf16))
    smalls, first = [], 0
    for one in small:
        smalls.append(packed[:, first : first + one.shape[0]].reshape(-1))
        first += one.shape[0]
    (
        query_add,
        value_add,
        offset_add,
        gain_one,
        shift_one,
        upward_add,
        downward_add,
        gain_two,
        shift_two,
    ) = smalls

    upward_full = lax.all_gather(upward_weight, EVERY, axis=0, tiled=True)
    downward_full = lax.all_gather(downward_weight, EVERY, axis=0, tiled=True)

    slopes = 2.0 ** (-8.0 * (jnp.arange(HEADS, dtype=f32) + 1.0) / HEADS) * (4.0 / (length * ns))
    slopes = lax.dynamic_slice_in_dim(slopes, seq * group, group)
    order = jnp.argsort(block_order[0]).astype(jnp.int32)

    inputs = tokens.reshape(length, features).astype(f32)
    normed, first_pull = jax.vjp(layer_norm, inputs, gain_one, shift_one)
    normed_low = normed.astype(bf16)
    zeros = jnp.zeros_like(query_add)
    bias = jnp.concatenate([query_add, zeros, value_add])
    joint_full, projection_full, mixture = joint_product(
        normed_low, joint_weight, bias, projection
    )
    pairs = len(mixture)
    slopes = slopes.reshape(pairs, 2)
    qkv = [over_seq(one) for one in mixture]
    forward = [attention_forward(qkv[pair], order, slopes[pair]) for pair in range(pairs)]
    attended = jnp.stack([over_seq(one[0]) for one in forward])
    attended_low = attended.transpose(2, 1, 0, 3).reshape(length, features)

    middle = inputs + matmul(attended_low, projection_full) + offset_add
    second, second_pull = jax.vjp(layer_norm, middle, gain_two, shift_two)
    second_low = second.astype(bf16)
    hidden = matmul(second_low, upward_full) + upward_add
    active, derivative = gelu_both(hidden)
    derivative = derivative.astype(bf16)
    active_low = active.astype(bf16)
    result = matmul(active_low, downward_full) + downward_add
    output = (middle + result).astype(bf16).reshape(members, length, features)

    grad_result = cotangent.reshape(length, features)
    grad_result_full = grad_result.astype(f32)
    downward_mine, downward_other = halves(active_low, grad_result)
    downwardbias_grad = jnp.sum(grad_result_full, 0)
    downward_other = to_core(downward_other)
    grad_active = right_transposed(after(grad_result, downward_mine), downward_full)
    grad_hidden = grad_active * derivative.astype(f32)
    grad_hidden_low = grad_hidden.astype(bf16)
    downward_chip = (downward_mine.astype(f32) + downward_other.astype(f32)).astype(bf16)
    downward_sum = lax.psum_scatter(
        downward_chip.reshape(ns * nz, -1, features), ("seq", "z"), scatter_dimension=0, tiled=True
    )[0].astype(f32)
    upward_mine, upward_other = halves(after(second_low, downward_chip), grad_hidden_low)
    upward_other = to_core(upward_other)
    upwardbias_grad = jnp.sum(grad_hidden_low.astype(f32), 0)
    grad_second = right_transposed(after(grad_hidden_low, upward_mine), upward_full)
    middle_part, secondgain_grad, secondshift_grad = second_pull(grad_second)

    grad_middle = grad_result_full + middle_part
    grad_branch = grad_middle.astype(bf16)
    offset_grad = jnp.sum(grad_branch.astype(f32), 0)
    grad_attended = right_transposed(grad_branch, projection_full).astype(bf16)
    grad_attended = grad_attended.reshape(length, ns, pairs, 128).transpose(2, 1, 0, 3)
    grad_attended = [over_seq(grad_attended[pair]) for pair in range(pairs)]
    projection_mine, projection_other = halves(attended_low, grad_branch)
    projection_other = to_core(projection_other)
    upward_terms = seq_step(upward_mine, upward_other, (projection_mine, projection_other))
    grad_attended[0] = after(grad_attended[0], upward_terms[0])
    upward_parts = column_sums(upward_terms)
    grad_qkv = []
    for pair in range(pairs):
        low, full, logs = forward[pair]
        grad = attention_backward(qkv[pair], grad_attended[pair], full, logs, order, slopes[pair])
        if pair == pairs - 1:
            grad = after(grad, upward_parts[0], downward_sum)
        grad_qkv.append(over_seq(grad))
    upward_sum = last_step(z_step(upward_parts))
    upward_sum, projection_sum = upward_sum[:, :-features], upward_sum[:, -features:]
    grad_qkv[0] = after(grad_qkv[0], upward_sum, output)
    joint_mine, joint_other = joint_halves(normed_low, grad_qkv)
    joint_terms = seq_step(joint_mine, to_core(joint_other))
    grad_qkv[0] = after(grad_qkv[0], joint_terms[0])
    mixture_sums = jnp.stack([jnp.sum(grad.astype(f32), 2) for grad in grad_qkv])
    mixture_sums = mixture_sums.transpose(2, 1, 0, 3).reshape(-1)
    grad_normed = joint_back(grad_qkv, joint_full)
    input_part, firstgain_grad, firstshift_grad = first_pull(grad_normed)
    input_grad = (grad_middle + input_part).astype(bf16).reshape(members, length, features)

    grads = (
        mixture_sums[:features],
        mixture_sums[2 * features :],
        offset_grad,
        firstgain_grad,
        firstshift_grad,
        upwardbias_grad,
        downwardbias_grad,
        secondgain_grad,
        secondshift_grad,
    )
    packed = jnp.concatenate([g.reshape(devices, -1) for g in grads], 1)
    packed = scattered_small(packed)
    joint_terms[0] = after(joint_terms[0], packed, input_grad)
    joint_sum = last_step(z_step(column_sums(joint_terms)))
    sums, first = [], 0
    for one in small:
        sums.append(packed[first : first + one.shape[0]])
        first += one.shape[0]
    return (
        output,
        input_grad,
        joint_sum,
        sums[0],
        sums[1],
        projection_sum,
        sums[2],
        sums[3],
        sums[4],
        upward_sum,
        sums[5],
        downward_sum,
        sums[6],
        sums[7],
        sums[8],
    )


def solution(mesh):
    ns, dp = mesh.devices.shape
    split = Mesh(mesh.devices.reshape(ns, dp // 2, 2), EVERY)
    tokens = P(("z", "core"), "seq", None)
    matrix = P(EVERY, None)
    vector = P(EVERY)
    orders = P(("z", "core"), None)
    kinds = (tokens, tokens, orders, matrix, vector, vector, matrix, vector, vector, vector)
    kinds += (matrix, vector, matrix, vector, vector, vector)
    in_specs = kinds
    out_specs = kinds[:2] + kinds[3:]
    return jax.shard_map(body, mesh=split, in_specs=in_specs, out_specs=out_specs, check_vma=False)
```

```python
import math
from functools import partial

import jax
import jax.numpy as jnp
from jax import lax
from jax.experimental import pallas as pl
from jax.experimental.pallas import tpu as pltpu
from jax.sharding import Mesh, PartitionSpec as P

HEADS = 16
EVERY = ("seq", "z", "core")
LOG2E = math.log2(math.e)
epsilon = 1e-05
lowest = -1e30
bf16 = jnp.bfloat16
f32 = jnp.float32


def layer_norm(values, scaling, shifting):
    average = jnp.mean(values, -1, keepdims=True)
    centered = values - average
    variance = jnp.mean(centered * centered, -1, keepdims=True)
    return centered * lax.rsqrt(variance + epsilon) * scaling + shifting


def gelu_both(values):
    slope = math.sqrt(2.0 / math.pi)
    square = values * values
    curve = jnp.tanh(slope * values * (1.0 + 0.044715 * square))
    half = 0.5 * (1.0 + curve)
    inner = slope * (1.0 + 3 * 0.044715 * square)
    return values * half, half + 0.5 * values * (1.0 - curve * curve) * inner


def matmul(left, right):
    return jnp.dot(left, right, preferred_element_type=f32)


def left_transposed(left, right):
    return lax.dot_general(left, right, (((0,), (0,)), ((), ())), preferred_element_type=f32)


def right_transposed(left, right):
    return lax.dot_general(left, right, (((1,), (1,)), ((), ())), preferred_element_type=f32)


def sizes():
    return lax.axis_size("seq"), lax.axis_size("z")


def places():
    return lax.axis_index("seq"), lax.axis_index("z"), lax.axis_index("core")


def to_core(value):
    return lax.ppermute(value, "core", [(0, 1), (1, 0)])


def to_seq(value, by):
    count = lax.axis_size("seq")
    return lax.ppermute(value, "seq", [(i, i ^ by) for i in range(count)])


def to_z(value, by):
    count = lax.axis_size("z")
    return lax.ppermute(value, "z", [(i, (i + by) % count) for i in range(count)])


def after(value, *others):
    return lax.optimization_barrier((value, *others))[0]


def along_z(value):
    return [value] + [to_z(value, by) for by in range(1, sizes()[1])]


def along_seq(value):
    return [value] + [to_seq(value, by) for by in range(1, sizes()[0])]


def with_core(pieces):
    return [p for piece in pieces for p in (piece, to_core(piece))]


def owner_seq_outer(nz):
    def owner(p, t, seq, z, core):
        return ((seq ^ (p // 2)) * nz + lax.rem(z - t + nz, nz)) * 2 + (core ^ (p % 2))

    return owner


def owner_z_outer(nz):
    def owner(p, t, seq, z, core):
        return ((seq ^ t) * nz + lax.rem(z - p // 2 + nz, nz)) * 2 + (core ^ (p % 2))

    return owner


def gathered_small(shard):
    ns, nz = sizes()
    seq, z, core = places()
    count = shard.shape[0]
    column = jnp.stack(along_z(shard))
    plane = jnp.stack(along_seq(column))
    both = jnp.stack([plane, to_core(plane)]).reshape(-1, count)
    device = jnp.arange(ns * nz * 2)
    s, t, c = device // (2 * nz), (device // 2) % nz, device % 2
    held_at = ((c ^ core) * ns + (s ^ seq)) * nz + (z - t + nz) % nz
    chosen = held_at[:, None] == jnp.arange(ns * nz * 2)[None]
    return matmul(chosen.astype(bf16), both)


def halves(left, right):
    ns, nz = sizes()
    tokens, depth = left.shape
    columns = right.shape[1]
    rows = depth // (ns * nz * 2)
    core = places()[2].astype(jnp.int32)
    if rows % 16:
        blocks = left_transposed(left, right).astype(bf16).reshape(ns, nz, 2, rows, columns)
        return (
            lax.dynamic_index_in_dim(blocks, core, 2, keepdims=False),
            lax.dynamic_index_in_dim(blocks, 1 - core, 2, keepdims=False),
        )
    tile = depth // ns

    def kernel(core_ref, left_ref, right_ref, mine_ref, other_ref):
        product = left_transposed(left_ref[...], right_ref[...]).astype(bf16)
        product = product.reshape(nz, 2, rows, columns)
        first = core_ref[0] == 0
        mine_ref[0] = jnp.where(first, product[:, 0], product[:, 1])
        other_ref[0] = jnp.where(first, product[:, 1], product[:, 0])

    out = pl.BlockSpec((1, nz, rows, columns), lambda i, core: (i, 0, 0, 0))
    return pl.pallas_call(
        kernel,
        name="halves",
        grid_spec=pltpu.PrefetchScalarGridSpec(
            num_scalar_prefetch=1,
            grid=(ns,),
            in_specs=[
                pl.BlockSpec((tokens, tile), lambda i, core: (0, i)),
                pl.BlockSpec((tokens, columns), lambda i, core: (0, 0)),
            ],
            out_specs=[out, out],
        ),
        out_shape=[jax.ShapeDtypeStruct((ns, nz, rows, columns), bf16)] * 2,
        compiler_params=pltpu.CompilerParams(vmem_limit_bytes=40 << 20),
        cost_estimate=pl.CostEstimate(
            flops=2 * tokens * depth * columns,
            bytes_accessed=2 * (tokens * (depth + columns) + depth * columns),
            transcendentals=0,
        ),
    )(core[None], left, right)


def joint_halves(left, rights):
    ns, nz = sizes()
    tokens, depth = left.shape
    pairs = len(rights)
    width = pairs * 128
    columns = 3 * ns * width
    rows = depth // (ns * nz * 2)
    if rows % 16:
        right = jnp.concatenate(rights, 3)
        return halves(left, right.transpose(2, 1, 0, 3).reshape(tokens, columns))
    tile = depth // ns

    def kernel(core_ref, left_ref, *refs):
        rights_ref, mine_ref, other_ref = refs[:pairs], *refs[pairs:]
        first = core_ref[0] == 0
        rows_left = left_ref[...].T
        for group in range(ns):
            for kind in range(3):
                at = (kind * ns + group) * width
                right = jnp.concatenate([ref[group, kind] for ref in rights_ref], 1)
                product = matmul(rows_left, right).astype(bf16)
                product = product.reshape(nz, 2, rows, width)
                mine_ref[0, :, :, at : at + width] = jnp.where(first, product[:, 0], product[:, 1])
                other_ref[0, :, :, at : at + width] = jnp.where(first, product[:, 1], product[:, 0])

    out = pl.BlockSpec((1, nz, rows, columns), lambda i, core: (i, 0, 0, 0))
    right = pl.BlockSpec((ns, 3, tokens, 128), lambda i, core: (0, 0, 0, 0))
    return pl.pallas_call(
        kernel,
        name="joint_halves",
        grid_spec=pltpu.PrefetchScalarGridSpec(
            num_scalar_prefetch=1,
            grid=(ns,),
            in_specs=[pl.BlockSpec((tokens, tile), lambda i, core: (0, i))] + [right] * pairs,
            out_specs=[out, out],
        ),
        out_shape=[jax.ShapeDtypeStruct((ns, nz, rows, columns), bf16)] * 2,
        compiler_params=pltpu.CompilerParams(vmem_limit_bytes=40 << 20),
        cost_estimate=pl.CostEstimate(
            flops=2 * tokens * depth * columns,
            bytes_accessed=2 * (tokens * (depth + columns) + depth * columns),
            transcendentals=0,
        ),
    )(places()[2].astype(jnp.int32)[None], left, *rights)


def joint_back(grads, weight):
    ns, _, tokens, _ = grads[0].shape
    pairs = len(grads)
    width = pairs * 128
    depth = weight.shape[0]

    def kernel(*refs):
        grads_ref, weight_ref, out_ref = refs[:pairs], *refs[pairs:]
        result = jnp.zeros((tokens, depth), f32)
        for group in range(ns):
            for kind in range(3):
                at = (kind * ns + group) * width
                grad = jnp.concatenate([ref[group, kind] for ref in grads_ref], 1)
                result += right_transposed(grad, weight_ref[:, at : at + width])
        out_ref[...] = result

    return pl.pallas_call(
        kernel,
        name="joint_back",
        out_shape=jax.ShapeDtypeStruct((tokens, depth), f32),
        compiler_params=pltpu.CompilerParams(vmem_limit_bytes=24 << 20),
        cost_estimate=pl.CostEstimate(flops=0, bytes_accessed=depth, transcendentals=0),
    )(*grads, weight)


def summed(terms, order, extra=()):
    n, m, rows, columns = terms[0].shape
    more = extra[0].shape[3] if extra else 0
    count, both = len(terms), len(terms) + len(extra)

    def kernel(order_ref, *refs):
        for k in range(n):
            ins, out = refs[k * both : (k + 1) * both], refs[n * both + k]
            for group, start, size in ((ins[:count], 0, columns), (ins[count:], columns, more)):
                if size:
                    result = group[0][0, 0].astype(f32)
                    for ref in group[1:]:
                        result = result + ref[0, 0].astype(f32)
                    out[0, :, start : start + size] = result.astype(bf16)

    def block(k, size):
        return pl.BlockSpec((1, 1, rows, size), lambda i, order: (order[k], i, 0, 0))

    in_specs = []
    for k in range(n):
        in_specs += [block(k, columns)] * count + [block(k, more)] * len(extra)
    total = columns + more
    return pl.pallas_call(
        kernel,
        name="summed",
        grid_spec=pltpu.PrefetchScalarGridSpec(
            num_scalar_prefetch=1,
            grid=(m,),
            in_specs=in_specs,
            out_specs=[pl.BlockSpec((1, rows, total), lambda i, order: (i, 0, 0))] * n,
        ),
        out_shape=[jax.ShapeDtypeStruct((m, rows, total), bf16)] * n,
        compiler_params=pltpu.CompilerParams(vmem_limit_bytes=32 << 20),
        cost_estimate=pl.CostEstimate(
            flops=0, bytes_accessed=(count + 1) * 2 * n * m * rows * total, transcendentals=0
        ),
    )(order.astype(jnp.int32), *([*terms, *extra] * n))


def added(left, right):
    n, m, rows, columns = left.shape

    def kernel(left_ref, right_ref, out_ref):
        out_ref[...] = (left_ref[...].astype(f32) + right_ref[...].astype(f32)).astype(bf16)

    block = pl.BlockSpec((1, m, rows, columns), lambda i: (i, 0, 0, 0))
    return pl.pallas_call(
        kernel,
        name="added",
        grid=(n,),
        in_specs=[block, block],
        out_specs=block,
        out_shape=jax.ShapeDtypeStruct(left.shape, bf16),
        compiler_params=pltpu.CompilerParams(vmem_limit_bytes=32 << 20),
        cost_estimate=pl.CostEstimate(
            flops=left.size, bytes_accessed=6 * left.size, transcendentals=0
        ),
    )(left, right)


def seq_step(mine, other, extra=()):
    ns = sizes()[0]
    if mine.shape[2] % 16:
        chip = mine.astype(f32) + other.astype(f32)
        if extra:
            chip = jnp.concatenate([chip, extra[0].astype(f32) + extra[1].astype(f32)], 3)
        return [chip.astype(bf16)]
    parts = summed([mine, other], places()[0] ^ jnp.arange(ns), extra)
    return [parts[0]] + [to_seq(parts[by], by) for by in range(1, ns)]


def column_sums(terms):
    if len(terms) == 1:
        return terms
    nz = sizes()[1]
    return summed([term[:, None] for term in terms], (places()[1] + jnp.arange(nz)) % nz)


def z_step(parts):
    if len(parts) == 1:
        return parts
    return [parts[0][0]] + [to_z(parts[by][0], by) for by in range(1, sizes()[1])]


def last_step(terms):
    if len(terms) == 1:
        chip = terms[0].reshape(-1, *terms[0].shape[2:])
        return lax.psum_scatter(chip, ("seq", "z"), scatter_dimension=0, tiled=True)[0].astype(f32)
    result = terms[0].astype(f32)
    for term in terms[1:]:
        result = result + term.astype(f32)
    return result


def over_seq(value):
    return lax.all_to_all(value, "seq", 0, 0, tiled=True)


def scattered_small(values):
    ns, nz = sizes()
    seq, z, core = places()
    blocks = values.reshape(ns, nz, 2, -1)

    def pick(array, index, axis):
        return lax.dynamic_index_in_dim(array, index, axis, keepdims=False)

    chip = pick(blocks, core, 2) + to_core(pick(blocks, 1 - core, 2))
    plane = pick(chip, seq, 0)
    for by in range(1, ns):
        plane = plane + to_seq(pick(chip, seq ^ by, 0), by)
    result = pick(plane, z, 0)
    for by in range(1, nz):
        result = result + to_z(pick(plane, (z + by) % nz, 0), by)
    return result


def joint_product(normed, shard, bias, later):
    ns, nz = sizes()
    tokens, features = normed.shape
    rows, columns = shard.shape
    width = features // ns
    pairs = width // 128
    if rows % 16:
        full = lax.all_gather(shard, EVERY, axis=0, tiled=True)
        last = lax.all_gather(later, EVERY, axis=0, tiled=True)
        mixture = (matmul(normed, full) + bias).astype(bf16)
        mixture = mixture.reshape(tokens, 3, ns, pairs, 128).transpose(3, 2, 1, 0, 4)
        return full, last, [mixture[pair] for pair in range(pairs)]
    one = jnp.stack(along_z(shard))
    two = after(jnp.stack(along_seq(later)), one)
    ones = with_core(along_seq(one))
    twos = with_core(along_z(two))
    owners = [owner_seq_outer(nz)] * len(ones) + [owner_z_outer(nz)] * len(twos)
    numbers = list(range(len(ones))) + list(range(len(twos)))
    pieces = ones + twos
    count = len(pieces)
    slots = sum(piece.shape[0] for piece in pieces)
    devices = slots // 2

    def kernel(place, *refs):
        ins = refs[:count]
        normed_ref, bias_ref, full_ref, last_ref = refs[count : count + 4]
        outs_ref = refs[count + 4 : count + 4 + pairs]
        held, held_last, in_sem, out_sem = refs[count + 4 + pairs :]
        copies = []
        for p in range(count):
            to = held if p < len(ones) else held_last
            for t in range(ins[p].shape[0]):
                device = owners[p](numbers[p], t, place[0], place[1], place[2])
                sem = in_sem.at[len(copies)]
                copy = pltpu.make_async_copy(ins[p].at[t], to.at[device], sem)
                copy.start()
                copies.append(copy)
        for copy in copies[:devices]:
            copy.wait()
        full_copy = pltpu.make_async_copy(held, full_ref, out_sem.at[0])
        full_copy.start()
        for kind in range(3):
            for group in range(ns):
                at = kind * features + group * width
                weight = held[:, :, at : at + width].reshape(features, width)
                product = matmul(normed_ref[...], weight) + bias_ref[:, at : at + width]
                product = product.astype(bf16)
                for pair in range(pairs):
                    outs_ref[pair][group, kind] = product[:, pair * 128 : pair * 128 + 128]
        for copy in copies[devices:]:
            copy.wait()
        last_copy = pltpu.make_async_copy(held_last, last_ref, out_sem.at[1])
        last_copy.start()
        full_copy.wait()
        last_copy.wait()

    place = jnp.stack(places()).astype(jnp.int32)
    anywhere = pl.BlockSpec(memory_space=pl.ANY)
    inside = pl.BlockSpec(memory_space=pltpu.VMEM)
    full, last, *mixture = pl.pallas_call(
        kernel,
        name="joint_product",
        out_shape=[
            jax.ShapeDtypeStruct((devices, rows, columns), bf16),
            jax.ShapeDtypeStruct((devices, *later.shape), bf16),
        ]
        + [jax.ShapeDtypeStruct((ns, 3, tokens, 128), bf16)] * pairs,
        in_specs=[pl.BlockSpec(memory_space=pltpu.SMEM)] + [anywhere] * count + [inside] * 2,
        out_specs=[anywhere, anywhere] + [inside] * pairs,
        scratch_shapes=[
            pltpu.VMEM((devices, rows, columns), bf16),
            pltpu.VMEM((devices, *later.shape), bf16),
            pltpu.SemaphoreType.DMA((slots,)),
            pltpu.SemaphoreType.DMA((2,)),
        ],
        compiler_params=pltpu.CompilerParams(vmem_limit_bytes=24 << 20),
        cost_estimate=pl.CostEstimate(
            flops=2 * tokens * features * columns,
            bytes_accessed=6 * features * columns,
            transcendentals=0,
        ),
    )(place, *pieces, normed, bias[None])
    return full.reshape(features, columns), last.reshape(features, -1), mixture


def half_lanes(shape, which):
    lane = lax.broadcasted_iota(jnp.int32, shape, len(shape) - 1)
    return (lane < 64) if which == 0 else (lane >= 64)


def with_bias(keys, slope, first_place, which):
    lane = lax.broadcasted_iota(jnp.int32, keys.shape, 1) - (64 if which == 0 else 0)
    row = lax.broadcasted_iota(jnp.int32, keys.shape, 0) + first_place
    bias = row.astype(f32) * (slope * 8.0)
    high = bias.astype(bf16)
    rest = bias - high.astype(f32)
    middle = rest.astype(bf16)
    low = (rest - middle.astype(f32)).astype(bf16)
    zero = jnp.zeros_like(high)
    terms = jnp.where(
        lane == 0, high, jnp.where(lane == 1, middle, jnp.where(lane == 2, low, zero))
    )
    return jnp.where(half_lanes(keys.shape, which), keys, terms)


def attention_forward(qkv, order, slopes):
    ns, _, length, width = qkv.shape
    pairs = width // 128
    scale = LOG2E / 8.0

    def kernel(order_ref, slope_ref, q_ref, kv_ref, low_ref, full_ref, log_ref):
        pair, place = pl.program_id(0), pl.program_id(1)
        shape = (length, 128)
        queries = [
            jnp.where(half_lanes(shape, w), q_ref[0, 0], jnp.ones(shape, bf16)) for w in (0, 1)
        ]

        def step(block, state, diagonal):
            at = order_ref[block]
            result = []
            for w in (0, 1):
                top, acc = state[w]
                keys = with_bias(kv_ref[at, 1], slope_ref[pair * 2 + w], block * length, w)
                scores = right_transposed(keys, queries[w])
                if diagonal:
                    k = lax.broadcasted_iota(jnp.int32, scores.shape, 0)
                    q = lax.broadcasted_iota(jnp.int32, scores.shape, 1)
                    scores = jnp.where(k <= q, scores, lowest)
                new_top = jnp.maximum(top, jnp.max(scores, 0, keepdims=True))
                weights = jnp.exp2(scores * scale - new_top * scale).astype(bf16)
                values = jnp.where(half_lanes(shape, w), kv_ref[at, 2], jnp.ones(shape, bf16))
                acc = acc * jnp.exp2((top - new_top) * scale) + left_transposed(values, weights)
                result.append((new_top, acc))
            return tuple(result)

        start = (jnp.full((1, length), lowest, f32), jnp.zeros((128, length), f32))
        state = lax.fori_loop(
            0, place, lambda block, state: step(block, state, False), (start, start)
        )
        (top0, acc0), (top1, acc1) = step(place, state, True)
        sum0, sum1 = acc0[64:65], acc1[0:1]
        row = lax.broadcasted_iota(jnp.int32, (128, length), 0)
        attended = jnp.where(row < 64, acc0 / sum0, acc1 / sum1).T
        full_ref[0] = attended
        low_ref[0] = attended.astype(bf16)
        row = lax.broadcasted_iota(jnp.int32, (8, length), 0)
        log_ref[0, 0] = jnp.where(
            row == 0, top0 * scale + jnp.log2(sum0), top1 * scale + jnp.log2(sum1)
        )

    per_block = 2 * 2 * length * length * 128 * 2
    grid_spec = pltpu.PrefetchScalarGridSpec(
        num_scalar_prefetch=2,
        grid=(pairs, ns),
        in_specs=[
            pl.BlockSpec((1, 1, length, 128), lambda p, i, order, slope: (order[i], 0, 0, p)),
            pl.BlockSpec((ns, 3, length, 128), lambda p, i, order, slope: (0, 0, 0, p)),
        ],
        out_specs=[
            pl.BlockSpec((1, length, 128), lambda p, i, order, slope: (order[i], 0, p)),
            pl.BlockSpec((1, length, 128), lambda p, i, order, slope: (order[i], 0, p)),
            pl.BlockSpec((1, 1, 8, length), lambda p, i, order, slope: (p, i, 0, 0)),
        ],
    )
    return pl.pallas_call(
        kernel,
        name="attention_forward",
        grid_spec=grid_spec,
        out_shape=[
            jax.ShapeDtypeStruct((ns, length, width), bf16),
            jax.ShapeDtypeStruct((ns, length, width), f32),
            jax.ShapeDtypeStruct((pairs, ns, 8, length), f32),
        ],
        compiler_params=pltpu.CompilerParams(vmem_limit_bytes=40 << 20),
        cost_estimate=pl.CostEstimate(
            flops=pairs * per_block * ns * (ns + 1) // 2 * 12,
            bytes_accessed=qkv.size * 2 + ns * length * width * 6,
            transcendentals=pairs * ns * (ns + 1) * length * length,
        ),
    )(order, slopes, qkv, qkv)


def attention_backward(qkv, grad, full, logs, order, slopes):
    ns, _, length, width = qkv.shape
    pairs = width // 128
    scale = LOG2E / 8.0

    def kernel(
        order_ref, slope_ref, qkv_ref, grad_ref, full_ref, log_ref, out_ref, dq_ref, delta_ref
    ):
        pair, block = pl.program_id(0), pl.program_id(1)
        shape = (length, 128)

        @pl.when(block == 0)
        def _():
            def one(i, _):
                at = order_ref[i]
                product = (grad_ref[at].astype(f32) * full_ref[at]).T
                delta_ref[i] = jnp.concatenate(
                    [
                        jnp.sum(product[:64], 0, keepdims=True),
                        jnp.sum(product[64:], 0, keepdims=True),
                    ],
                    0,
                )
                dq_ref[i] = jnp.zeros((128, length), f32)
                return 0

            lax.fori_loop(0, ns, one, 0)

        here = order_ref[block]
        keys, values = qkv_ref[here, 1], qkv_ref[here, 2]
        zero = jnp.zeros(shape, bf16)
        one = jnp.ones(shape, bf16)
        masks = [half_lanes(shape, w) for w in (0, 1)]
        biased = [
            with_bias(keys, slope_ref[pair * 2 + w], block * length, w) for w in (0, 1)
        ]
        own_keys = [jnp.where(masks[w], keys, zero) for w in (0, 1)]
        own_values = [jnp.where(masks[w], values, zero) for w in (0, 1)]

        def step(i, state, diagonal):
            at = order_ref[i]
            grad_keys, grad_values = state
            queries, grads = qkv_ref[at, 0], grad_ref[at]
            grad_queries = dq_ref[i]
            for w in (0, 1):
                scores = right_transposed(biased[w], jnp.where(masks[w], queries, one))
                weights = jnp.exp2(scores * scale - log_ref[0, i, w : w + 1])
                if diagonal:
                    k = lax.broadcasted_iota(jnp.int32, scores.shape, 0)
                    q = lax.broadcasted_iota(jnp.int32, scores.shape, 1)
                    weights = jnp.where(k <= q, weights, 0.0)
                grad_weights = right_transposed(own_values[w], grads)
                grad_scores = (weights * (grad_weights - delta_ref[i, w : w + 1])).astype(bf16)
                own_grads = jnp.where(masks[w], grads, zero)
                own_queries = jnp.where(masks[w], queries, zero)
                grad_values = grad_values + matmul(weights.astype(bf16), own_grads)
                grad_keys = grad_keys + matmul(grad_scores, own_queries)
                grad_queries = grad_queries + left_transposed(own_keys[w], grad_scores)
            dq_ref[i] = grad_queries
            return grad_keys, grad_values

        start = (jnp.zeros(shape, f32), jnp.zeros(shape, f32))
        state = step(block, start, True)
        grad_keys, grad_values = lax.fori_loop(
            block + 1, ns, lambda i, state: step(i, state, False), state
        )
        out_ref[here, 1] = (grad_keys * 0.125).astype(bf16)
        out_ref[here, 2] = grad_values.astype(bf16)
        out_ref[here, 0] = (dq_ref[block].T * 0.125).astype(bf16)

    per_block = 2 * 5 * length * length * 128 * 2
    grid_spec = pltpu.PrefetchScalarGridSpec(
        num_scalar_prefetch=2,
        grid=(pairs, ns),
        in_specs=[
            pl.BlockSpec((ns, 3, length, 128), lambda p, i, order, slope: (0, 0, 0, p)),
            pl.BlockSpec((ns, length, 128), lambda p, i, order, slope: (0, 0, p)),
            pl.BlockSpec((ns, length, 128), lambda p, i, order, slope: (0, 0, p)),
            pl.BlockSpec((1, ns, 8, length), lambda p, i, order, slope: (p, 0, 0, 0)),
        ],
        out_specs=pl.BlockSpec((ns, 3, length, 128), lambda p, i, order, slope: (0, 0, 0, p)),
        scratch_shapes=[
            pltpu.VMEM((ns, 128, length), f32),
            pltpu.VMEM((ns, 2, length), f32),
        ],
    )
    return pl.pallas_call(
        kernel,
        name="attention_backward",
        grid_spec=grid_spec,
        out_shape=jax.ShapeDtypeStruct((ns, 3, length, width), bf16),
        compiler_params=pltpu.CompilerParams(vmem_limit_bytes=48 << 20),
        cost_estimate=pl.CostEstimate(
            flops=pairs * per_block * ns * (ns + 1) // 2 * 5,
            bytes_accessed=qkv.size * 4 + ns * length * width * 6,
            transcendentals=pairs * ns * (ns + 1) * length * length,
        ),
    )(order, slopes, qkv, grad, full, logs)


def dense_call(kernel, name, grid, in_specs, out_specs, out_shape, flops, moved):
    return pl.pallas_call(
        kernel,
        name=name,
        grid=grid,
        in_specs=in_specs,
        out_specs=out_specs,
        out_shape=out_shape,
        compiler_params=pltpu.CompilerParams(vmem_limit_bytes=24 << 20),
        cost_estimate=pl.CostEstimate(flops=flops, bytes_accessed=moved, transcendentals=0),
    )


def whole(shape):
    return pl.BlockSpec(shape, lambda i: (0,) * len(shape))


def hidden_step(second, weight, bias):
    tokens, features = second.shape
    hidden = weight.shape[1]
    block = min(hidden, 512)

    def kernel(second_ref, weight_ref, bias_ref, active_ref, derivative_ref):
        active, derivative = gelu_both(matmul(second_ref[...], weight_ref[...]) + bias_ref[...])
        active_ref[...] = active.astype(bf16)
        derivative_ref[...] = derivative.astype(bf16)

    out = pl.BlockSpec((tokens, block), lambda i: (0, i))
    return dense_call(
        kernel,
        "hidden_step",
        (hidden // block,),
        [
            whole((tokens, features)),
            pl.BlockSpec((features, block), lambda i: (0, i)),
            pl.BlockSpec((1, block), lambda i: (0, i)),
        ],
        [out, out],
        [jax.ShapeDtypeStruct((tokens, hidden), bf16)] * 2,
        2 * tokens * weight.size,
        2 * weight.size + 4 * tokens * hidden,
    )(second, weight, bias[None])


def hidden_back(grad, weight, derivative):
    tokens, features = grad.shape
    hidden = weight.shape[0]
    block = min(hidden, 512)

    def kernel(grad_ref, weight_ref, derivative_ref, out_ref, sum_ref):
        product = right_transposed(grad_ref[...], weight_ref[...])
        product = (product * derivative_ref[...].astype(f32)).astype(bf16)
        out_ref[...] = product
        sum_ref[...] = jnp.sum(product.astype(f32), 0, keepdims=True)

    return dense_call(
        kernel,
        "hidden_back",
        (hidden // block,),
        [
            whole((tokens, features)),
            pl.BlockSpec((block, features), lambda i: (i, 0)),
            pl.BlockSpec((tokens, block), lambda i: (0, i)),
        ],
        [
            pl.BlockSpec((tokens, block), lambda i: (0, i)),
            pl.BlockSpec((1, block), lambda i: (0, i)),
        ],
        [
            jax.ShapeDtypeStruct((tokens, hidden), bf16),
            jax.ShapeDtypeStruct((1, hidden), f32),
        ],
        2 * tokens * weight.size,
        2 * weight.size + 4 * tokens * hidden,
    )(grad, weight, derivative)


def projected(attended, weight):
    ns, tokens, _ = attended[0].shape
    pairs = len(attended)
    features = weight.shape[0]
    width = pairs * 128

    def kernel(*refs):
        parts, weight_ref, low_ref, out_ref = refs[:pairs], *refs[pairs:]
        result = jnp.zeros(out_ref.shape, f32)
        for group in range(ns):
            rows = jnp.concatenate([part[group] for part in parts], 1)
            low_ref[:, group * width : (group + 1) * width] = rows
            result += matmul(rows, weight_ref[group * width : (group + 1) * width, :])
        out_ref[...] = result

    return dense_call(
        kernel,
        "projected",
        (1,),
        [whole((ns, tokens, 128))] * pairs + [whole(weight.shape)],
        [whole((tokens, features)), whole((tokens, weight.shape[1]))],
        [
            jax.ShapeDtypeStruct((tokens, features), bf16),
            jax.ShapeDtypeStruct((tokens, weight.shape[1]), f32),
        ],
        2 * tokens * weight.size,
        2 * weight.size + 8 * tokens * features,
    )(*attended, weight)


def projected_back(grad, weight, ns):
    tokens, features = grad.shape
    width = weight.shape[0] // ns
    pairs = width // 128

    def kernel(grad_ref, weight_ref, *parts):
        for group in range(ns):
            rows = weight_ref[group * width : (group + 1) * width, :]
            product = right_transposed(grad_ref[...], rows).astype(bf16)
            for pair in range(pairs):
                parts[pair][group] = product[:, pair * 128 : pair * 128 + 128]

    return dense_call(
        kernel,
        "projected_back",
        (1,),
        [whole((tokens, features)), whole(weight.shape)],
        [whole((ns, tokens, 128))] * pairs,
        [jax.ShapeDtypeStruct((ns, tokens, 128), bf16)] * pairs,
        2 * tokens * weight.size,
        2 * weight.size + 4 * tokens * features,
    )(grad, weight)


def body(
    tokens,
    cotangent,
    block_order,
    joint_weight,
    query_bias,
    value_bias,
    projection,
    offset,
    first_gain,
    first_shift,
    upward_weight,
    upward_bias,
    downward_weight,
    downward_bias,
    second_gain,
    second_shift,
):
    members, length, features = tokens.shape
    ns, nz = sizes()
    seq = lax.axis_index("seq")
    width = features // ns
    group = HEADS // ns
    devices = ns * nz * 2

    small = (
        query_bias,
        value_bias,
        offset,
        first_gain,
        first_shift,
        upward_bias,
        downward_bias,
        second_gain,
        second_shift,
    )
    sizes_small = [one.shape[0] for one in small]
    count = sum(sizes_small)
    packed, first = jnp.zeros((count,), f32), 0
    for one in small:
        packed += jnp.pad(one.astype(f32), (first, count - first - one.shape[0]))
        first += one.shape[0]
    packed = gathered_small(packed.astype(bf16))
    smalls, first = [], 0
    for one in small:
        smalls.append(packed[:, first : first + one.shape[0]].reshape(-1))
        first += one.shape[0]
    (
        query_add,
        value_add,
        offset_add,
        gain_one,
        shift_one,
        upward_add,
        downward_add,
        gain_two,
        shift_two,
    ) = smalls

    upward_full = lax.all_gather(upward_weight, EVERY, axis=0, tiled=True)
    downward_full = lax.all_gather(downward_weight, EVERY, axis=0, tiled=True)

    slopes = 2.0 ** (-8.0 * (jnp.arange(HEADS, dtype=f32) + 1.0) / HEADS) * (4.0 / (length * ns))
    slopes = lax.dynamic_slice_in_dim(slopes, seq * group, group)
    order = jnp.argsort(block_order[0]).astype(jnp.int32)

    inputs = tokens.reshape(length, features).astype(f32)
    normed, first_pull = jax.vjp(layer_norm, inputs, gain_one, shift_one)
    normed_low = normed.astype(bf16)
    zeros = jnp.zeros_like(query_add)
    bias = jnp.concatenate([query_add, zeros, value_add])
    joint_full, projection_full, mixture = joint_product(
        normed_low, joint_weight, bias, projection
    )
    pairs = len(mixture)
    slopes = slopes.reshape(pairs, 2)
    qkv = [over_seq(one) for one in mixture]
    forward = [attention_forward(qkv[pair], order, slopes[pair]) for pair in range(pairs)]
    attended = [over_seq(one[0]) for one in forward]
    attended_low, branch = projected(attended, projection_full)

    middle = inputs + branch + offset_add
    second, second_pull = jax.vjp(layer_norm, middle, gain_two, shift_two)
    second_low = second.astype(bf16)
    active_low, derivative = hidden_step(second_low, upward_full, upward_add)
    result = matmul(active_low, downward_full) + downward_add
    output = (middle + result).astype(bf16).reshape(members, length, features)

    grad_result = cotangent.reshape(length, features)
    grad_result_full = grad_result.astype(f32)
    downward_mine, downward_other = halves(active_low, grad_result)
    downwardbias_grad = jnp.sum(grad_result_full, 0)
    downward_other = to_core(downward_other)
    grad_hidden_low, upwardbias_grad = hidden_back(
        after(grad_result, downward_mine), downward_full, derivative
    )
    upwardbias_grad = upwardbias_grad[0]
    downward_chip = added(downward_mine, downward_other)
    downward_sum = lax.psum_scatter(
        downward_chip.reshape(ns * nz, -1, features), ("seq", "z"), scatter_dimension=0, tiled=True
    )[0].astype(f32)
    upward_mine, upward_other = halves(after(second_low, downward_chip), grad_hidden_low)
    upward_other = to_core(upward_other)
    grad_second = right_transposed(after(grad_hidden_low, upward_mine), upward_full)
    middle_part, secondgain_grad, secondshift_grad = second_pull(grad_second)

    grad_middle = grad_result_full + middle_part
    grad_branch = grad_middle.astype(bf16)
    offset_grad = jnp.sum(grad_branch.astype(f32), 0)
    grad_attended = [over_seq(part) for part in projected_back(grad_branch, projection_full, ns)]
    projection_mine, projection_other = halves(attended_low, grad_branch)
    projection_other = to_core(projection_other)
    upward_terms = seq_step(upward_mine, upward_other, (projection_mine, projection_other))
    grad_attended[0] = after(grad_attended[0], upward_terms[0])
    upward_parts = column_sums(upward_terms)
    grad_qkv = []
    for pair in range(pairs):
        low, full, logs = forward[pair]
        grad = attention_backward(qkv[pair], grad_attended[pair], full, logs, order, slopes[pair])
        if pair == pairs - 1:
            grad = after(grad, upward_parts[0], downward_sum)
        grad_qkv.append(over_seq(grad))
    upward_sum = last_step(z_step(upward_parts))
    upward_sum, projection_sum = upward_sum[:, :-features], upward_sum[:, -features:]
    grad_qkv[0] = after(grad_qkv[0], upward_sum, output)
    joint_mine, joint_other = joint_halves(normed_low, grad_qkv)
    joint_terms = seq_step(joint_mine, to_core(joint_other))
    grad_qkv[0] = after(grad_qkv[0], joint_terms[0])
    mixture_sums = jnp.stack([jnp.sum(grad.astype(f32), 2) for grad in grad_qkv])
    mixture_sums = mixture_sums.transpose(2, 1, 0, 3).reshape(-1)
    grad_normed = joint_back(grad_qkv, joint_full)
    input_part, firstgain_grad, firstshift_grad = first_pull(grad_normed)
    input_grad = (grad_middle + input_part).astype(bf16).reshape(members, length, features)

    grads = (
        mixture_sums[:features],
        mixture_sums[2 * features :],
        offset_grad,
        firstgain_grad,
        firstshift_grad,
        upwardbias_grad,
        downwardbias_grad,
        secondgain_grad,
        secondshift_grad,
    )
    packed = jnp.concatenate([g.reshape(devices, -1) for g in grads], 1)
    packed = scattered_small(packed)
    joint_terms[0] = after(joint_terms[0], packed, input_grad)
    joint_sum = last_step(z_step(column_sums(joint_terms)))
    sums, first = [], 0
    for one in small:
        sums.append(packed[first : first + one.shape[0]])
        first += one.shape[0]
    return (
        output,
        input_grad,
        joint_sum,
        sums[0],
        sums[1],
        projection_sum,
        sums[2],
        sums[3],
        sums[4],
        upward_sum,
        sums[5],
        downward_sum,
        sums[6],
        sums[7],
        sums[8],
    )


def solution(mesh):
    ns, dp = mesh.devices.shape
    split = Mesh(mesh.devices.reshape(ns, dp // 2, 2), EVERY)
    tokens = P(("z", "core"), "seq", None)
    matrix = P(EVERY, None)
    vector = P(EVERY)
    orders = P(("z", "core"), None)
    kinds = (tokens, tokens, orders, matrix, vector, vector, matrix, vector, vector, vector)
    kinds += (matrix, vector, matrix, vector, vector, vector)
    in_specs = kinds
    out_specs = kinds[:2] + kinds[3:]
    return jax.shard_map(body, mesh=split, in_specs=in_specs, out_specs=out_specs, check_vma=False)
```

```python
import math
from functools import partial

import jax
import jax.numpy as jnp
from jax import lax
from jax.experimental import pallas as pl
from jax.experimental.pallas import tpu as pltpu
from jax.sharding import Mesh, PartitionSpec as P

HEADS = 16
EVERY = ("seq", "z", "core")
LOG2E = math.log2(math.e)
epsilon = 1e-05
lowest = -1e30
bf16 = jnp.bfloat16
f32 = jnp.float32


def layer_norm(values, scaling, shifting):
    average = jnp.mean(values, -1, keepdims=True)
    centered = values - average
    variance = jnp.mean(centered * centered, -1, keepdims=True)
    return centered * lax.rsqrt(variance + epsilon) * scaling + shifting


def gelu_both(values):
    slope = math.sqrt(2.0 / math.pi)
    square = values * values
    curve = jnp.tanh(slope * values * (1.0 + 0.044715 * square))
    half = 0.5 * (1.0 + curve)
    inner = slope * (1.0 + 3 * 0.044715 * square)
    return values * half, half + 0.5 * values * (1.0 - curve * curve) * inner


def matmul(left, right):
    return jnp.dot(left, right, preferred_element_type=f32)


def left_transposed(left, right):
    return lax.dot_general(left, right, (((0,), (0,)), ((), ())), preferred_element_type=f32)


def right_transposed(left, right):
    return lax.dot_general(left, right, (((1,), (1,)), ((), ())), preferred_element_type=f32)


def sizes():
    return lax.axis_size("seq"), lax.axis_size("z")


def places():
    return lax.axis_index("seq"), lax.axis_index("z"), lax.axis_index("core")


def to_core(value):
    return lax.ppermute(value, "core", [(0, 1), (1, 0)])


def to_seq(value, by):
    count = lax.axis_size("seq")
    return lax.ppermute(value, "seq", [(i, i ^ by) for i in range(count)])


def to_z(value, by):
    count = lax.axis_size("z")
    return lax.ppermute(value, "z", [(i, (i + by) % count) for i in range(count)])


def after(value, *others):
    return lax.optimization_barrier((value, *others))[0]


def along_z(value):
    return [value] + [to_z(value, by) for by in range(1, sizes()[1])]


def along_seq(value):
    return [value] + [to_seq(value, by) for by in range(1, sizes()[0])]


def with_core(pieces):
    return [p for piece in pieces for p in (piece, to_core(piece))]


def owner_seq_outer(nz):
    def owner(p, t, seq, z, core):
        return ((seq ^ (p // 2)) * nz + lax.rem(z - t + nz, nz)) * 2 + (core ^ (p % 2))

    return owner


def owner_z_outer(nz):
    def owner(p, t, seq, z, core):
        return ((seq ^ t) * nz + lax.rem(z - p // 2 + nz, nz)) * 2 + (core ^ (p % 2))

    return owner


def gathered_small(shard):
    ns, nz = sizes()
    seq, z, core = places()
    count = shard.shape[0]
    column = jnp.stack(along_z(shard))
    plane = jnp.stack(along_seq(column))
    both = jnp.stack([plane, to_core(plane)]).reshape(-1, count)
    device = jnp.arange(ns * nz * 2)
    s, t, c = device // (2 * nz), (device // 2) % nz, device % 2
    held_at = ((c ^ core) * ns + (s ^ seq)) * nz + (z - t + nz) % nz
    chosen = held_at[:, None] == jnp.arange(ns * nz * 2)[None]
    return matmul(chosen.astype(bf16), both)


def halves(left, right):
    ns, nz = sizes()
    tokens, depth = left.shape
    columns = right.shape[1]
    rows = depth // (ns * nz * 2)
    core = places()[2].astype(jnp.int32)
    if rows % 16:
        blocks = left_transposed(left, right).astype(bf16).reshape(ns, nz, 2, rows, columns)
        return (
            lax.dynamic_index_in_dim(blocks, core, 2, keepdims=False),
            lax.dynamic_index_in_dim(blocks, 1 - core, 2, keepdims=False),
        )
    tile = depth // ns

    def kernel(core_ref, left_ref, right_ref, mine_ref, other_ref):
        product = left_transposed(left_ref[...], right_ref[...]).astype(bf16)
        product = product.reshape(nz, 2, rows, columns)
        first = core_ref[0] == 0
        mine_ref[0] = jnp.where(first, product[:, 0], product[:, 1])
        other_ref[0] = jnp.where(first, product[:, 1], product[:, 0])

    out = pl.BlockSpec((1, nz, rows, columns), lambda i, core: (i, 0, 0, 0))
    return pl.pallas_call(
        kernel,
        name="halves",
        grid_spec=pltpu.PrefetchScalarGridSpec(
            num_scalar_prefetch=1,
            grid=(ns,),
            in_specs=[
                pl.BlockSpec((tokens, tile), lambda i, core: (0, i)),
                pl.BlockSpec((tokens, columns), lambda i, core: (0, 0)),
            ],
            out_specs=[out, out],
        ),
        out_shape=[jax.ShapeDtypeStruct((ns, nz, rows, columns), bf16)] * 2,
        compiler_params=pltpu.CompilerParams(vmem_limit_bytes=40 << 20),
        cost_estimate=pl.CostEstimate(
            flops=2 * tokens * depth * columns,
            bytes_accessed=2 * (tokens * (depth + columns) + depth * columns),
            transcendentals=0,
        ),
    )(core[None], left, right)


def joint_halves(left, rights):
    ns, nz = sizes()
    tokens, depth = left.shape
    pairs = len(rights)
    width = pairs * 128
    columns = 3 * ns * width
    rows = depth // (ns * nz * 2)
    if rows % 16:
        right = jnp.concatenate(rights, 3)
        return halves(left, right.transpose(2, 1, 0, 3).reshape(tokens, columns))
    tile = depth // ns

    def kernel(core_ref, left_ref, *refs):
        rights_ref, mine_ref, other_ref = refs[:pairs], *refs[pairs:]
        first = core_ref[0] == 0
        rows_left = left_ref[...].T
        for group in range(ns):
            for kind in range(3):
                at = (kind * ns + group) * width
                right = jnp.concatenate([ref[group, kind] for ref in rights_ref], 1)
                product = matmul(rows_left, right).astype(bf16)
                product = product.reshape(nz, 2, rows, width)
                mine_ref[0, :, :, at : at + width] = jnp.where(first, product[:, 0], product[:, 1])
                other_ref[0, :, :, at : at + width] = jnp.where(first, product[:, 1], product[:, 0])

    out = pl.BlockSpec((1, nz, rows, columns), lambda i, core: (i, 0, 0, 0))
    right = pl.BlockSpec((ns, 3, tokens, 128), lambda i, core: (0, 0, 0, 0))
    return pl.pallas_call(
        kernel,
        name="joint_halves",
        grid_spec=pltpu.PrefetchScalarGridSpec(
            num_scalar_prefetch=1,
            grid=(ns,),
            in_specs=[pl.BlockSpec((tokens, tile), lambda i, core: (0, i))] + [right] * pairs,
            out_specs=[out, out],
        ),
        out_shape=[jax.ShapeDtypeStruct((ns, nz, rows, columns), bf16)] * 2,
        compiler_params=pltpu.CompilerParams(vmem_limit_bytes=40 << 20),
        cost_estimate=pl.CostEstimate(
            flops=2 * tokens * depth * columns,
            bytes_accessed=2 * (tokens * (depth + columns) + depth * columns),
            transcendentals=0,
        ),
    )(places()[2].astype(jnp.int32)[None], left, *rights)


def joint_back(grads, weight):
    ns, _, tokens, _ = grads[0].shape
    pairs = len(grads)
    width = pairs * 128
    depth = weight.shape[0]

    def kernel(*refs):
        grads_ref, weight_ref, out_ref = refs[:pairs], *refs[pairs:]
        result = jnp.zeros((tokens, depth), f32)
        for group in range(ns):
            for kind in range(3):
                at = (kind * ns + group) * width
                grad = jnp.concatenate([ref[group, kind] for ref in grads_ref], 1)
                result += right_transposed(grad, weight_ref[:, at : at + width])
        out_ref[...] = result

    return pl.pallas_call(
        kernel,
        name="joint_back",
        out_shape=jax.ShapeDtypeStruct((tokens, depth), f32),
        compiler_params=pltpu.CompilerParams(vmem_limit_bytes=24 << 20),
        cost_estimate=pl.CostEstimate(flops=0, bytes_accessed=depth, transcendentals=0),
    )(*grads, weight)


def summed(terms, order, extra=()):
    n, m, rows, columns = terms[0].shape
    more = extra[0].shape[3] if extra else 0
    count, both = len(terms), len(terms) + len(extra)

    def kernel(order_ref, *refs):
        for k in range(n):
            ins, out = refs[k * both : (k + 1) * both], refs[n * both + k]
            for group, start, size in ((ins[:count], 0, columns), (ins[count:], columns, more)):
                if size:
                    result = group[0][0, 0].astype(f32)
                    for ref in group[1:]:
                        result = result + ref[0, 0].astype(f32)
                    out[0, :, start : start + size] = result.astype(bf16)

    def block(k, size):
        return pl.BlockSpec((1, 1, rows, size), lambda i, order: (order[k], i, 0, 0))

    in_specs = []
    for k in range(n):
        in_specs += [block(k, columns)] * count + [block(k, more)] * len(extra)
    total = columns + more
    return pl.pallas_call(
        kernel,
        name="summed",
        grid_spec=pltpu.PrefetchScalarGridSpec(
            num_scalar_prefetch=1,
            grid=(m,),
            in_specs=in_specs,
            out_specs=[pl.BlockSpec((1, rows, total), lambda i, order: (i, 0, 0))] * n,
        ),
        out_shape=[jax.ShapeDtypeStruct((m, rows, total), bf16)] * n,
        compiler_params=pltpu.CompilerParams(vmem_limit_bytes=32 << 20),
        cost_estimate=pl.CostEstimate(
            flops=0, bytes_accessed=(count + 1) * 2 * n * m * rows * total, transcendentals=0
        ),
    )(order.astype(jnp.int32), *([*terms, *extra] * n))


def added(left, right):
    n, m, rows, columns = left.shape

    def kernel(left_ref, right_ref, out_ref):
        out_ref[...] = (left_ref[...].astype(f32) + right_ref[...].astype(f32)).astype(bf16)

    block = pl.BlockSpec((1, m, rows, columns), lambda i: (i, 0, 0, 0))
    return pl.pallas_call(
        kernel,
        name="added",
        grid=(n,),
        in_specs=[block, block],
        out_specs=block,
        out_shape=jax.ShapeDtypeStruct(left.shape, bf16),
        compiler_params=pltpu.CompilerParams(vmem_limit_bytes=32 << 20),
        cost_estimate=pl.CostEstimate(
            flops=left.size, bytes_accessed=6 * left.size, transcendentals=0
        ),
    )(left, right)


def seq_step(mine, other, extra=()):
    ns = sizes()[0]
    if mine.shape[2] % 16:
        chip = mine.astype(f32) + other.astype(f32)
        if extra:
            chip = jnp.concatenate([chip, extra[0].astype(f32) + extra[1].astype(f32)], 3)
        return [chip.astype(bf16)]
    parts = summed([mine, other], places()[0] ^ jnp.arange(ns), extra)
    return [parts[0]] + [to_seq(parts[by], by) for by in range(1, ns)]


def column_sums(terms):
    if len(terms) == 1:
        return terms
    nz = sizes()[1]
    return summed([term[:, None] for term in terms], (places()[1] + jnp.arange(nz)) % nz)


def z_step(parts):
    if len(parts) == 1:
        return parts
    return [parts[0][0]] + [to_z(parts[by][0], by) for by in range(1, sizes()[1])]


def last_step(terms):
    if len(terms) == 1:
        chip = terms[0].reshape(-1, *terms[0].shape[2:])
        return lax.psum_scatter(chip, ("seq", "z"), scatter_dimension=0, tiled=True)[0].astype(f32)
    result = terms[0].astype(f32)
    for term in terms[1:]:
        result = result + term.astype(f32)
    return result


def over_seq(value):
    return lax.all_to_all(value, "seq", 0, 0, tiled=True)


def scattered_small(values):
    ns, nz = sizes()
    seq, z, core = places()
    blocks = values.reshape(ns, nz, 2, -1)

    def pick(array, index, axis):
        return lax.dynamic_index_in_dim(array, index, axis, keepdims=False)

    chip = pick(blocks, core, 2) + to_core(pick(blocks, 1 - core, 2))
    plane = pick(chip, seq, 0)
    for by in range(1, ns):
        plane = plane + to_seq(pick(chip, seq ^ by, 0), by)
    result = pick(plane, z, 0)
    for by in range(1, nz):
        result = result + to_z(pick(plane, (z + by) % nz, 0), by)
    return result


def joint_product(normed, shard, bias, later):
    ns, nz = sizes()
    tokens, features = normed.shape
    rows, columns = shard.shape
    width = features // ns
    pairs = width // 128
    if rows % 16:
        full = lax.all_gather(shard, EVERY, axis=0, tiled=True)
        last = lax.all_gather(later, EVERY, axis=0, tiled=True)
        mixture = (matmul(normed, full) + bias).astype(bf16)
        mixture = mixture.reshape(tokens, 3, ns, pairs, 128).transpose(3, 2, 1, 0, 4)
        return full, last, [mixture[pair] for pair in range(pairs)]
    one = jnp.stack(along_z(shard))
    two = after(jnp.stack(along_seq(later)), one)
    ones = with_core(along_seq(one))
    twos = with_core(along_z(two))
    owners = [owner_seq_outer(nz)] * len(ones) + [owner_z_outer(nz)] * len(twos)
    numbers = list(range(len(ones))) + list(range(len(twos)))
    pieces = ones + twos
    count = len(pieces)
    slots = sum(piece.shape[0] for piece in pieces)
    devices = slots // 2

    def kernel(place, *refs):
        ins = refs[:count]
        normed_ref, bias_ref, full_ref, last_ref = refs[count : count + 4]
        outs_ref = refs[count + 4 : count + 4 + pairs]
        held, held_last, in_sem, out_sem = refs[count + 4 + pairs :]
        copies = []
        for p in range(count):
            to = held if p < len(ones) else held_last
            for t in range(ins[p].shape[0]):
                device = owners[p](numbers[p], t, place[0], place[1], place[2])
                sem = in_sem.at[len(copies)]
                copy = pltpu.make_async_copy(ins[p].at[t], to.at[device], sem)
                copy.start()
                copies.append(copy)
        for copy in copies[:devices]:
            copy.wait()
        full_copy = pltpu.make_async_copy(held, full_ref, out_sem.at[0])
        full_copy.start()
        for kind in range(3):
            for group in range(ns):
                at = kind * features + group * width
                weight = held[:, :, at : at + width].reshape(features, width)
                product = matmul(normed_ref[...], weight) + bias_ref[:, at : at + width]
                product = product.astype(bf16)
                for pair in range(pairs):
                    outs_ref[pair][group, kind] = product[:, pair * 128 : pair * 128 + 128]
        for copy in copies[devices:]:
            copy.wait()
        last_copy = pltpu.make_async_copy(held_last, last_ref, out_sem.at[1])
        last_copy.start()
        full_copy.wait()
        last_copy.wait()

    place = jnp.stack(places()).astype(jnp.int32)
    anywhere = pl.BlockSpec(memory_space=pl.ANY)
    inside = pl.BlockSpec(memory_space=pltpu.VMEM)
    full, last, *mixture = pl.pallas_call(
        kernel,
        name="joint_product",
        out_shape=[
            jax.ShapeDtypeStruct((devices, rows, columns), bf16),
            jax.ShapeDtypeStruct((devices, *later.shape), bf16),
        ]
        + [jax.ShapeDtypeStruct((ns, 3, tokens, 128), bf16)] * pairs,
        in_specs=[pl.BlockSpec(memory_space=pltpu.SMEM)] + [anywhere] * count + [inside] * 2,
        out_specs=[anywhere, anywhere] + [inside] * pairs,
        scratch_shapes=[
            pltpu.VMEM((devices, rows, columns), bf16),
            pltpu.VMEM((devices, *later.shape), bf16),
            pltpu.SemaphoreType.DMA((slots,)),
            pltpu.SemaphoreType.DMA((2,)),
        ],
        compiler_params=pltpu.CompilerParams(vmem_limit_bytes=24 << 20),
        cost_estimate=pl.CostEstimate(
            flops=2 * tokens * features * columns,
            bytes_accessed=6 * features * columns,
            transcendentals=0,
        ),
    )(place, *pieces, normed, bias[None])
    return full.reshape(features, columns), last.reshape(features, -1), mixture


def half_lanes(shape, which):
    lane = lax.broadcasted_iota(jnp.int32, shape, len(shape) - 1)
    return (lane < 64) if which == 0 else (lane >= 64)


def with_bias(keys, slope, first_place, which):
    lane = lax.broadcasted_iota(jnp.int32, keys.shape, 1) - (64 if which == 0 else 0)
    row = lax.broadcasted_iota(jnp.int32, keys.shape, 0) + first_place
    bias = row.astype(f32) * (slope * 8.0)
    high = bias.astype(bf16)
    rest = bias - high.astype(f32)
    middle = rest.astype(bf16)
    low = (rest - middle.astype(f32)).astype(bf16)
    zero = jnp.zeros_like(high)
    terms = jnp.where(
        lane == 0, high, jnp.where(lane == 1, middle, jnp.where(lane == 2, low, zero))
    )
    return jnp.where(half_lanes(keys.shape, which), keys, terms)


def attention_forward(qkv, order, slopes):
    ns, _, length, width = qkv.shape
    pairs = width // 128
    scale = LOG2E / 8.0

    def kernel(order_ref, slope_ref, q_ref, kv_ref, low_ref, full_ref, log_ref):
        pair, place = pl.program_id(0), pl.program_id(1)
        shape = (length, 128)
        queries = [
            jnp.where(half_lanes(shape, w), q_ref[0, 0], jnp.ones(shape, bf16)) for w in (0, 1)
        ]

        def step(block, state, diagonal):
            at = order_ref[block]
            result = []
            for w in (0, 1):
                top, acc = state[w]
                keys = with_bias(kv_ref[at, 1], slope_ref[pair * 2 + w], block * length, w)
                scores = right_transposed(keys, queries[w])
                if diagonal:
                    k = lax.broadcasted_iota(jnp.int32, scores.shape, 0)
                    q = lax.broadcasted_iota(jnp.int32, scores.shape, 1)
                    scores = jnp.where(k <= q, scores, lowest)
                new_top = jnp.maximum(top, jnp.max(scores, 0, keepdims=True))
                weights = jnp.exp2(scores * scale - new_top * scale).astype(bf16)
                values = jnp.where(half_lanes(shape, w), kv_ref[at, 2], jnp.ones(shape, bf16))
                acc = acc * jnp.exp2((top - new_top) * scale) + left_transposed(values, weights)
                result.append((new_top, acc))
            return tuple(result)

        start = (jnp.full((1, length), lowest, f32), jnp.zeros((128, length), f32))
        state = lax.fori_loop(
            0, place, lambda block, state: step(block, state, False), (start, start)
        )
        (top0, acc0), (top1, acc1) = step(place, state, True)
        sum0, sum1 = acc0[64:65], acc1[0:1]
        row = lax.broadcasted_iota(jnp.int32, (128, length), 0)
        attended = jnp.where(row < 64, acc0 / sum0, acc1 / sum1).T
        full_ref[0] = attended
        low_ref[0] = attended.astype(bf16)
        row = lax.broadcasted_iota(jnp.int32, (8, length), 0)
        log_ref[0, 0] = jnp.where(
            row == 0, top0 * scale + jnp.log2(sum0), top1 * scale + jnp.log2(sum1)
        )

    per_block = 2 * 2 * length * length * 128 * 2
    grid_spec = pltpu.PrefetchScalarGridSpec(
        num_scalar_prefetch=2,
        grid=(pairs, ns),
        in_specs=[
            pl.BlockSpec((1, 1, length, 128), lambda p, i, order, slope: (order[i], 0, 0, p)),
            pl.BlockSpec((ns, 3, length, 128), lambda p, i, order, slope: (0, 0, 0, p)),
        ],
        out_specs=[
            pl.BlockSpec((1, length, 128), lambda p, i, order, slope: (order[i], 0, p)),
            pl.BlockSpec((1, length, 128), lambda p, i, order, slope: (order[i], 0, p)),
            pl.BlockSpec((1, 1, 8, length), lambda p, i, order, slope: (p, i, 0, 0)),
        ],
    )
    return pl.pallas_call(
        kernel,
        name="attention_forward",
        grid_spec=grid_spec,
        out_shape=[
            jax.ShapeDtypeStruct((ns, length, width), bf16),
            jax.ShapeDtypeStruct((ns, length, width), f32),
            jax.ShapeDtypeStruct((pairs, ns, 8, length), f32),
        ],
        compiler_params=pltpu.CompilerParams(vmem_limit_bytes=40 << 20),
        cost_estimate=pl.CostEstimate(
            flops=pairs * per_block * ns * (ns + 1) // 2 * 12,
            bytes_accessed=qkv.size * 2 + ns * length * width * 6,
            transcendentals=pairs * ns * (ns + 1) * length * length,
        ),
    )(order, slopes, qkv, qkv)


def attention_backward(qkv, grad, full, logs, order, slopes):
    ns, _, length, width = qkv.shape
    pairs = width // 128
    scale = LOG2E / 8.0

    def kernel(
        order_ref, slope_ref, qkv_ref, grad_ref, full_ref, log_ref, out_ref, dq_ref, delta_ref
    ):
        pair, block = pl.program_id(0), pl.program_id(1)
        shape = (length, 128)

        @pl.when(block == 0)
        def _():
            def one(i, _):
                at = order_ref[i]
                product = (grad_ref[at].astype(f32) * full_ref[at]).T
                delta_ref[i] = jnp.concatenate(
                    [
                        jnp.sum(product[:64], 0, keepdims=True),
                        jnp.sum(product[64:], 0, keepdims=True),
                    ],
                    0,
                )
                dq_ref[i] = jnp.zeros((128, length), f32)
                return 0

            lax.fori_loop(0, ns, one, 0)

        here = order_ref[block]
        keys, values = qkv_ref[here, 1], qkv_ref[here, 2]
        zero = jnp.zeros(shape, bf16)
        one = jnp.ones(shape, bf16)
        masks = [half_lanes(shape, w) for w in (0, 1)]
        biased = [
            with_bias(keys, slope_ref[pair * 2 + w], block * length, w) for w in (0, 1)
        ]
        own_keys = [jnp.where(masks[w], keys, zero) for w in (0, 1)]
        own_values = [jnp.where(masks[w], values, zero) for w in (0, 1)]

        def step(i, state, diagonal):
            at = order_ref[i]
            grad_keys, grad_values = state
            queries, grads = qkv_ref[at, 0], grad_ref[at]
            grad_queries = dq_ref[i]
            for w in (0, 1):
                scores = right_transposed(biased[w], jnp.where(masks[w], queries, one))
                weights = jnp.exp2(scores * scale - log_ref[0, i, w : w + 1])
                if diagonal:
                    k = lax.broadcasted_iota(jnp.int32, scores.shape, 0)
                    q = lax.broadcasted_iota(jnp.int32, scores.shape, 1)
                    weights = jnp.where(k <= q, weights, 0.0)
                grad_weights = right_transposed(own_values[w], grads)
                grad_scores = (weights * (grad_weights - delta_ref[i, w : w + 1])).astype(bf16)
                own_grads = jnp.where(masks[w], grads, zero)
                own_queries = jnp.where(masks[w], queries, zero)
                grad_values = grad_values + matmul(weights.astype(bf16), own_grads)
                grad_keys = grad_keys + matmul(grad_scores, own_queries)
                grad_queries = grad_queries + left_transposed(own_keys[w], grad_scores)
            dq_ref[i] = grad_queries
            return grad_keys, grad_values

        start = (jnp.zeros(shape, f32), jnp.zeros(shape, f32))
        state = step(block, start, True)
        grad_keys, grad_values = lax.fori_loop(
            block + 1, ns, lambda i, state: step(i, state, False), state
        )
        out_ref[here, 1] = (grad_keys * 0.125).astype(bf16)
        out_ref[here, 2] = grad_values.astype(bf16)
        out_ref[here, 0] = (dq_ref[block].T * 0.125).astype(bf16)

    per_block = 2 * 5 * length * length * 128 * 2
    grid_spec = pltpu.PrefetchScalarGridSpec(
        num_scalar_prefetch=2,
        grid=(pairs, ns),
        in_specs=[
            pl.BlockSpec((ns, 3, length, 128), lambda p, i, order, slope: (0, 0, 0, p)),
            pl.BlockSpec((ns, length, 128), lambda p, i, order, slope: (0, 0, p)),
            pl.BlockSpec((ns, length, 128), lambda p, i, order, slope: (0, 0, p)),
            pl.BlockSpec((1, ns, 8, length), lambda p, i, order, slope: (p, 0, 0, 0)),
        ],
        out_specs=pl.BlockSpec((ns, 3, length, 128), lambda p, i, order, slope: (0, 0, 0, p)),
        scratch_shapes=[
            pltpu.VMEM((ns, 128, length), f32),
            pltpu.VMEM((ns, 2, length), f32),
        ],
    )
    return pl.pallas_call(
        kernel,
        name="attention_backward",
        grid_spec=grid_spec,
        out_shape=jax.ShapeDtypeStruct((ns, 3, length, width), bf16),
        compiler_params=pltpu.CompilerParams(vmem_limit_bytes=48 << 20),
        cost_estimate=pl.CostEstimate(
            flops=pairs * per_block * ns * (ns + 1) // 2 * 5,
            bytes_accessed=qkv.size * 4 + ns * length * width * 6,
            transcendentals=pairs * ns * (ns + 1) * length * length,
        ),
    )(order, slopes, qkv, grad, full, logs)


def dense_call(kernel, name, grid, in_specs, out_specs, out_shape, flops, moved):
    return pl.pallas_call(
        kernel,
        name=name,
        grid=grid,
        in_specs=in_specs,
        out_specs=out_specs,
        out_shape=out_shape,
        compiler_params=pltpu.CompilerParams(vmem_limit_bytes=24 << 20),
        cost_estimate=pl.CostEstimate(flops=flops, bytes_accessed=moved, transcendentals=0),
    )


def whole(shape):
    return pl.BlockSpec(shape, lambda i: (0,) * len(shape))


def hidden_step(second, weight, bias):
    tokens, features = second.shape
    hidden = weight.shape[1]
    block = min(hidden, 512)

    def kernel(second_ref, weight_ref, bias_ref, active_ref, derivative_ref):
        active, derivative = gelu_both(matmul(second_ref[...], weight_ref[...]) + bias_ref[...])
        active_ref[...] = active.astype(bf16)
        derivative_ref[...] = derivative.astype(bf16)

    out = pl.BlockSpec((tokens, block), lambda i: (0, i))
    return dense_call(
        kernel,
        "hidden_step",
        (hidden // block,),
        [
            whole((tokens, features)),
            pl.BlockSpec((features, block), lambda i: (0, i)),
            pl.BlockSpec((1, block), lambda i: (0, i)),
        ],
        [out, out],
        [jax.ShapeDtypeStruct((tokens, hidden), bf16)] * 2,
        2 * tokens * weight.size,
        2 * weight.size + 4 * tokens * hidden,
    )(second, weight, bias[None])


def hidden_back(grad, weight, derivative):
    tokens, features = grad.shape
    hidden = weight.shape[0]
    block = min(hidden, 512)

    def kernel(grad_ref, weight_ref, derivative_ref, out_ref, sum_ref):
        product = right_transposed(grad_ref[...], weight_ref[...])
        product = (product * derivative_ref[...].astype(f32)).astype(bf16)
        out_ref[...] = product
        sum_ref[...] = jnp.sum(product.astype(f32), 0, keepdims=True)

    return dense_call(
        kernel,
        "hidden_back",
        (hidden // block,),
        [
            whole((tokens, features)),
            pl.BlockSpec((block, features), lambda i: (i, 0)),
            pl.BlockSpec((tokens, block), lambda i: (0, i)),
        ],
        [
            pl.BlockSpec((tokens, block), lambda i: (0, i)),
            pl.BlockSpec((1, block), lambda i: (0, i)),
        ],
        [
            jax.ShapeDtypeStruct((tokens, hidden), bf16),
            jax.ShapeDtypeStruct((1, hidden), f32),
        ],
        2 * tokens * weight.size,
        2 * weight.size + 4 * tokens * hidden,
    )(grad, weight, derivative)


def projected(attended, weight):
    ns, tokens, width = attended.shape
    features = weight.shape[0]

    def kernel(attended_ref, weight_ref, low_ref, out_ref):
        result = jnp.zeros(out_ref.shape, f32)
        for group in range(ns):
            rows = attended_ref[group]
            low_ref[:, group * width : (group + 1) * width] = rows
            result += matmul(rows, weight_ref[group * width : (group + 1) * width, :])
        out_ref[...] = result

    return dense_call(
        kernel,
        "projected",
        (1,),
        [whole((ns, tokens, width)), whole(weight.shape)],
        [whole((tokens, features)), whole((tokens, weight.shape[1]))],
        [
            jax.ShapeDtypeStruct((tokens, features), bf16),
            jax.ShapeDtypeStruct((tokens, weight.shape[1]), f32),
        ],
        2 * tokens * weight.size,
        2 * weight.size + 8 * tokens * features,
    )(attended, weight)


def projected_back(grad, weight, ns):
    tokens, features = grad.shape
    width = weight.shape[0] // ns
    pairs = width // 128

    def kernel(grad_ref, weight_ref, *parts):
        for group in range(ns):
            rows = weight_ref[group * width : (group + 1) * width, :]
            product = right_transposed(grad_ref[...], rows).astype(bf16)
            for pair in range(pairs):
                parts[pair][group] = product[:, pair * 128 : pair * 128 + 128]

    return dense_call(
        kernel,
        "projected_back",
        (1,),
        [whole((tokens, features)), whole(weight.shape)],
        [whole((ns, tokens, 128))] * pairs,
        [jax.ShapeDtypeStruct((ns, tokens, 128), bf16)] * pairs,
        2 * tokens * weight.size,
        2 * weight.size + 4 * tokens * features,
    )(grad, weight)


def body(
    tokens,
    cotangent,
    block_order,
    joint_weight,
    query_bias,
    value_bias,
    projection,
    offset,
    first_gain,
    first_shift,
    upward_weight,
    upward_bias,
    downward_weight,
    downward_bias,
    second_gain,
    second_shift,
):
    members, length, features = tokens.shape
    ns, nz = sizes()
    seq = lax.axis_index("seq")
    width = features // ns
    group = HEADS // ns
    devices = ns * nz * 2

    small = (
        query_bias,
        value_bias,
        offset,
        first_gain,
        first_shift,
        upward_bias,
        downward_bias,
        second_gain,
        second_shift,
    )
    sizes_small = [one.shape[0] for one in small]
    count = sum(sizes_small)
    packed, first = jnp.zeros((count,), f32), 0
    for one in small:
        packed += jnp.pad(one.astype(f32), (first, count - first - one.shape[0]))
        first += one.shape[0]
    packed = gathered_small(packed.astype(bf16))
    smalls, first = [], 0
    for one in small:
        smalls.append(packed[:, first : first + one.shape[0]].reshape(-1))
        first += one.shape[0]
    (
        query_add,
        value_add,
        offset_add,
        gain_one,
        shift_one,
        upward_add,
        downward_add,
        gain_two,
        shift_two,
    ) = smalls

    upward_full = lax.all_gather(upward_weight, EVERY, axis=0, tiled=True)
    downward_full = lax.all_gather(downward_weight, EVERY, axis=0, tiled=True)

    slopes = 2.0 ** (-8.0 * (jnp.arange(HEADS, dtype=f32) + 1.0) / HEADS) * (4.0 / (length * ns))
    slopes = lax.dynamic_slice_in_dim(slopes, seq * group, group)
    order = jnp.argsort(block_order[0]).astype(jnp.int32)

    inputs = tokens.reshape(length, features).astype(f32)
    normed, first_pull = jax.vjp(layer_norm, inputs, gain_one, shift_one)
    normed_low = normed.astype(bf16)
    zeros = jnp.zeros_like(query_add)
    bias = jnp.concatenate([query_add, zeros, value_add])
    joint_full, projection_full, mixture = joint_product(
        normed_low, joint_weight, bias, projection
    )
    pairs = len(mixture)
    slopes = slopes.reshape(pairs, 2)
    qkv = [over_seq(one) for one in mixture]
    forward = [attention_forward(qkv[pair], order, slopes[pair]) for pair in range(pairs)]
    attended = over_seq(jnp.concatenate([one[0] for one in forward], 2))
    attended_low, branch = projected(attended, projection_full)

    middle = inputs + branch + offset_add
    second, second_pull = jax.vjp(layer_norm, middle, gain_two, shift_two)
    second_low = second.astype(bf16)
    active_low, derivative = hidden_step(second_low, upward_full, upward_add)
    result = matmul(active_low, downward_full) + downward_add
    output = (middle + result).astype(bf16).reshape(members, length, features)

    grad_result = cotangent.reshape(length, features)
    grad_result_full = grad_result.astype(f32)
    downward_mine, downward_other = halves(active_low, grad_result)
    downwardbias_grad = jnp.sum(grad_result_full, 0)
    downward_other = to_core(downward_other)
    grad_hidden_low, upwardbias_grad = hidden_back(
        after(grad_result, downward_mine), downward_full, derivative
    )
    upwardbias_grad = upwardbias_grad[0]
    downward_chip = added(downward_mine, downward_other)
    downward_sum = lax.psum_scatter(
        downward_chip.reshape(ns * nz, -1, features), ("seq", "z"), scatter_dimension=0, tiled=True
    )[0].astype(f32)
    upward_mine, upward_other = halves(after(second_low, downward_chip), grad_hidden_low)
    upward_other = to_core(upward_other)
    grad_second = right_transposed(after(grad_hidden_low, upward_mine), upward_full)
    middle_part, secondgain_grad, secondshift_grad = second_pull(grad_second)

    grad_middle = grad_result_full + middle_part
    grad_branch = grad_middle.astype(bf16)
    offset_grad = jnp.sum(grad_branch.astype(f32), 0)
    grad_attended = [over_seq(part) for part in projected_back(grad_branch, projection_full, ns)]
    projection_mine, projection_other = halves(attended_low, grad_branch)
    projection_other = to_core(projection_other)
    upward_terms = seq_step(upward_mine, upward_other, (projection_mine, projection_other))
    grad_attended[0] = after(grad_attended[0], upward_terms[0])
    upward_parts = column_sums(upward_terms)
    grad_qkv = []
    for pair in range(pairs):
        low, full, logs = forward[pair]
        grad = attention_backward(qkv[pair], grad_attended[pair], full, logs, order, slopes[pair])
        if pair == pairs - 1:
            grad = after(grad, upward_parts[0], downward_sum)
        grad_qkv.append(over_seq(grad))
    upward_sum = last_step(z_step(upward_parts))
    upward_sum, projection_sum = upward_sum[:, :-features], upward_sum[:, -features:]
    grad_qkv[0] = after(grad_qkv[0], upward_sum, output)
    joint_mine, joint_other = joint_halves(normed_low, grad_qkv)
    joint_terms = seq_step(joint_mine, to_core(joint_other))
    grad_qkv[0] = after(grad_qkv[0], joint_terms[0])
    mixture_sums = jnp.stack([jnp.sum(grad.astype(f32), 2) for grad in grad_qkv])
    mixture_sums = mixture_sums.transpose(2, 1, 0, 3).reshape(-1)
    grad_normed = joint_back(grad_qkv, joint_full)
    input_part, firstgain_grad, firstshift_grad = first_pull(grad_normed)
    input_grad = (grad_middle + input_part).astype(bf16).reshape(members, length, features)

    grads = (
        mixture_sums[:features],
        mixture_sums[2 * features :],
        offset_grad,
        firstgain_grad,
        firstshift_grad,
        upwardbias_grad,
        downwardbias_grad,
        secondgain_grad,
        secondshift_grad,
    )
    packed = jnp.concatenate([g.reshape(devices, -1) for g in grads], 1)
    packed = scattered_small(packed)
    joint_terms[0] = after(joint_terms[0], packed, input_grad)
    joint_sum = last_step(z_step(column_sums(joint_terms)))
    sums, first = [], 0
    for one in small:
        sums.append(packed[first : first + one.shape[0]])
        first += one.shape[0]
    return (
        output,
        input_grad,
        joint_sum,
        sums[0],
        sums[1],
        projection_sum,
        sums[2],
        sums[3],
        sums[4],
        upward_sum,
        sums[5],
        downward_sum,
        sums[6],
        sums[7],
        sums[8],
    )


def solution(mesh):
    ns, dp = mesh.devices.shape
    split = Mesh(mesh.devices.reshape(ns, dp // 2, 2), EVERY)
    tokens = P(("z", "core"), "seq", None)
    matrix = P(EVERY, None)
    vector = P(EVERY)
    orders = P(("z", "core"), None)
    kinds = (tokens, tokens, orders, matrix, vector, vector, matrix, vector, vector, vector)
    kinds += (matrix, vector, matrix, vector, vector, vector)
    in_specs = kinds
    out_specs = kinds[:2] + kinds[3:]
    return jax.shard_map(body, mesh=split, in_specs=in_specs, out_specs=out_specs, check_vma=False)
```
